32 devices in a mesh: tok: 16 (over z, y, core), feat: 2 (over x).
Axes of the slice: x: 2, y: 2, z: 4, core: 2. Of those that a mesh axis runs over, the one named last changes fastest.
Arguments:
- activations: bfloat16 [8192, 16384], P('tok', 'feat'), may hold values from -300 to 300
- down_proj: bfloat16 [16384, 1024], P('feat', 'tok'), may hold values from -0.00048828125 to 0.00048828125
- precond: bfloat16 [1024, 1024], replicated, may hold values from -1 to 2, as said below
- target: bfloat16 [8192, 256], P('tok'), may hold values from -8 to 8
Outputs:
- solution: float32 [1024, 256], P('feat')
- residual: float32 [8192, 256], P('tok')
The draws below stay inside these ranges and needn't reach their ends.
Inputs may be any that keep to these rules, and one draw needn't show every extreme that they name: `precond`: upper triangular.
All inputs are finite; a program needn't handle non-finite values.
Results may differ from the reference program's by a relative error of at most 0.025.
Values may be sent and summed in bfloat16 or wider, within the bound.
A program may use at most 64 MiB of HBM per device.

```python
import math
import jax
import jax.numpy as jnp
from jax import lax

H = 16384
R = 1024
K = 256
ITERS = 2
TOKENS = 8192


def draw_activations(key, part):
    key = jax.random.fold_in(key, 11)
    subkeys = jax.random.split(key, 3)
    growth = 3.0 ** (jnp.arange(TOKENS, dtype=jnp.float32) / TOKENS)
    entries = jnp.clip(jax.random.normal(subkeys[0], (TOKENS, H), jnp.float32), -5.0, 5.0)
    spread = 3.3
    row_scale = growth * jnp.exp(jax.random.uniform(subkeys[1], (TOKENS,), jnp.float32) * math.log(spread))
    col_scale = jnp.exp(jax.random.uniform(subkeys[2], (H,), jnp.float32, math.log(0.5), math.log(2.0)))
    return (entries * row_scale[:, None] * col_scale[None, :]).astype(jnp.bfloat16)


def draw_precond(key, part):
    key = jax.random.fold_in(key, 23)
    subkeys = jax.random.split(key, 2)
    diagonal = jnp.exp(jax.random.uniform(subkeys[0], (R,), jnp.float32, math.log(0.5), math.log(2.0)))
    offdiag = jnp.clip(jax.random.normal(subkeys[1], (R, R), jnp.float32), -4.0, 4.0)
    upper = jnp.triu(offdiag * (0.6 / math.sqrt(R)), 1)
    return (upper + jnp.diag(diagonal)).astype(jnp.bfloat16)


def shard_levels(key, extent, shards, smallest, largest):
    gain = 1.0
    for dim, blocks in shards:
        steps = jax.random.uniform(jax.random.fold_in(jax.random.fold_in(key, 6), dim), (blocks,), jnp.float32, smallest / len(shards), largest / len(shards))
        gain = gain * jnp.repeat(jnp.exp(steps), extent[dim] // blocks).reshape((-1,) + (1,) * (len(extent) - 1 - dim))
    return gain


def bell_draw(key, extent, width, reach, cuts=(), kind=jnp.bfloat16):
    drawn = width * jax.random.normal(key, extent, jnp.float32)
    if cuts:
        drawn = drawn * shard_levels(key, extent, cuts, -0.22, 0.18)
    return jnp.clip(drawn, -reach, reach).astype(kind)


def setup_inputs(seed: int = 0) -> dict:
    key_list = jax.random.split(jax.random.key(seed), 5)
    return {
        "activations": draw_activations(jax.random.fold_in(key_list[4], 71), 0),
        "down_proj": bell_draw(key_list[1], (H, R), (H * TOKENS) ** -0.5, 0.00048828125, ((0, 2), (1, 16))),
        "precond": draw_precond(jax.random.fold_in(key_list[4], 71), 0),
        "target": bell_draw(key_list[3], (TOKENS, K), 2.0, 8.0, ((0, 16),)),
    }


precise = lax.Precision.HIGHEST

def solve_gram(matrix, right):
    lower = jnp.linalg.cholesky(matrix)
    middle = lax.linalg.triangular_solve(lower, right, left_side=True, lower=True)
    return lax.linalg.triangular_solve(lower, middle, left_side=True, lower=True, transpose_a=True)

def reference(activations, down_proj, precond, target):
    joined = jnp.dot(activations.astype(jnp.float32), down_proj.astype(jnp.float32), preferred_element_type=jnp.float32).astype(jnp.bfloat16)

    def gradient(current):
        backed = jnp.dot(joined.T.astype(jnp.float32), current.astype(jnp.bfloat16).astype(jnp.float32), preferred_element_type=jnp.float32)
        return jnp.dot(precond.T.astype(jnp.float32), backed.astype(jnp.bfloat16).astype(jnp.float32), preferred_element_type=jnp.float32)
    residual = target.astype(jnp.float32)
    descent = gradient(residual)
    gram_now = jnp.dot(descent.T, descent, precision=precise)
    direction = descent
    solution = jnp.zeros((R, K), jnp.float32)
    for iteration in range(ITERS):
        lift = jnp.dot(precond.astype(jnp.float32), direction.astype(jnp.bfloat16).astype(jnp.float32), preferred_element_type=jnp.float32)
        image_now = jnp.dot(joined.astype(jnp.float32), lift.astype(jnp.bfloat16).astype(jnp.float32), preferred_element_type=jnp.float32)
        curvature = jnp.dot(image_now.T, image_now, precision=precise)
        step_size = solve_gram(curvature, gram_now)
        solution = solution + jnp.dot(lift, step_size, precision=precise)
        residual = residual - jnp.dot(image_now, step_size, precision=precise)
        if iteration + 1 < ITERS:
            descent = gradient(residual)
            gram_next = jnp.dot(descent.T, descent, precision=precise)
            mixing = solve_gram(gram_now, gram_next)
            direction = descent + jnp.dot(direction, mixing, precision=precise)
            gram_now = gram_next
    return (solution, residual)
```

```python
import functools

import jax
import jax.numpy as jnp
from jax import lax
from jax.experimental import pallas as pl
from jax.experimental.pallas import tpu as pltpu
from jax.sharding import PartitionSpec as P

ITERS = 2
Z, Y, CORES = 4, 2, 2
BLOCK = 256
DEPTH = 1024
MESH = pl.DeviceIdType.MESH
precise = lax.Precision.HIGHEST


def spread(buf, send, recv, on_slab):
    me = lax.axis_index("tok")
    z, y, c = me // (Y * CORES), (me // CORES) % Y, me % CORES

    def index(zz, yy, cc):
        return (zz * Y + yy) * CORES + cc

    targets = (me + Y * CORES, me - Y * CORES, index(z, 1 - y, c), index(z, y, 1 - c))

    def copy(i, way):
        return pltpu.make_async_remote_copy(
            src_ref=buf.at[i],
            dst_ref=buf.at[i],
            send_sem=send.at[way, i],
            recv_sem=recv.at[i],
            device_id={"tok": targets[way]},
            device_id_type=MESH,
        )

    def along(distance, visit):
        for sign in (1, -1) if distance else (1,):
            zz = z + sign * distance

            @pl.when((zz >= 0) & (zz < Z))
            def _():
                visit(zz, sign)

    def onward(i, zz, sign, act):
        if sign != 1 or zz is z:

            @pl.when(z < Z - 1)
            def _():
                act(copy(i, 0))

        if sign == 1:

            @pl.when(z > 0)
            def _():
                act(copy(i, 1))

        act(copy(i, 2))
        act(copy(i, 3))

    onward(me, z, 1, lambda k: k.start())
    for stage in range(Z):

        def line(zz, sign):
            i = index(zz, y, c)
            copy(i, 2).wait_recv()
            onward(i, zz, sign, lambda k: k.start())

        def side(zz, sign):
            i = index(zz, 1 - y, c)
            copy(i, 2).wait_recv()
            copy(i, 3).start()

        def slab(zz, sign):
            copy(index(zz, y, 1 - c), 3).wait_recv()
            copy(index(zz, 1 - y, 1 - c), 3).wait_recv()
            if on_slab is not None:
                on_slab(zz)

        if stage + 1 < Z:
            along(stage + 1, line)
        along(stage, side)
        along(stage, slab)

    onward(me, z, 1, lambda k: k.wait_send())
    for stage in range(Z):
        if stage:
            along(stage, lambda zz, sign: onward(index(zz, y, c), zz, sign, lambda k: k.wait_send()))
        along(stage, lambda zz, sign: copy(index(zz, 1 - y, c), 3).wait_send())


def pairs(slabs):
    upper = [(i, j) for i in range(slabs) for j in range(i, slabs)]
    return upper + [(i, None) for i in range(slabs)]


def reduce_kernel(
    a_ref, d_ref, t_ref, j_ref, m_ref,
    a_buf, d_buf, total, mine, theirs, out_buf, in_buf, all_buf,
    a_sem, d_sem, d_send, d_recv, x_send, x_recv, r_send, r_recv, p_send, p_recv, m_send, m_recv,
):
    me, feat = lax.axis_index("tok"), lax.axis_index("feat")
    count = Z * Y * CORES
    group = Y * CORES

    load_a = pltpu.make_async_copy(a_ref, a_buf, a_sem)
    load_d = pltpu.make_async_copy(d_ref, d_buf.at[me], d_sem)
    load_d.start()
    load_a.start()

    barrier = pltpu.get_barrier_semaphore()
    for step in range(1, count):
        pl.semaphore_signal(
            barrier, inc=1, device_id={"tok": lax.rem(me + step, count)}, device_id_type=MESH
        )
    pl.semaphore_signal(barrier, inc=1, device_id={"feat": 1 - feat}, device_id_type=MESH)
    pl.semaphore_wait(barrier, count)
    load_d.wait()

    def swap(slab):
        return pltpu.make_async_remote_copy(
            src_ref=mine.at[slab],
            dst_ref=theirs.at[slab],
            send_sem=x_send.at[slab],
            recv_sem=x_recv.at[slab],
            device_id={"feat": 1 - feat},
            device_id_type=MESH,
        )

    def project(slab):
        total[...] = jnp.zeros_like(total)

        def part(k, carry):
            columns = pl.ds(pl.multiple_of(k * DEPTH, DEPTH), DEPTH)
            weights = d_buf[pl.ds(slab * group, group), :, columns].reshape(BLOCK, DEPTH)
            total[...] += lax.dot_general(
                a_buf[:, columns], weights, (((1,), (1,)), ((), ())), preferred_element_type=jnp.float32
            )
            return carry

        lax.fori_loop(0, a_buf.shape[1] // DEPTH, part, 0)
        mine[slab] = total[...].astype(jnp.bfloat16)
        swap(slab).start()

    load_a.wait()
    spread(d_buf, d_send, d_recv, project)
    for slab in range(Z):
        swap(slab).wait()
        j_ref[slab] = (mine[slab].astype(jnp.float32) + theirs[slab].astype(jnp.float32)).astype(
            jnp.bfloat16
        )

    blocks = pairs(Z)
    half = len(blocks) // 2
    rows = BLOCK // count
    for owner in range(2):

        @pl.when(feat == owner)
        def _():
            for n, (i, j) in enumerate(blocks[owner * half : (owner + 1) * half]):
                product = lax.dot_general(
                    j_ref[i],
                    t_ref[...] if j is None else j_ref[j],
                    (((0,), (0,)), ((), ())),
                    preferred_element_type=jnp.float32,
                )
                out_buf[:, n] = product.astype(jnp.bfloat16).reshape(count, rows, BLOCK)

    def send_part(step):
        other = lax.rem(me + step, count)
        return pltpu.make_async_remote_copy(
            src_ref=out_buf.at[other],
            dst_ref=in_buf.at[me],
            send_sem=r_send.at[step],
            recv_sem=r_recv.at[me],
            device_id={"tok": other},
            device_id_type=MESH,
        )

    def take_part(step):
        other = lax.rem(me + step, count)
        pltpu.make_async_remote_copy(
            src_ref=out_buf.at[other],
            dst_ref=in_buf.at[other],
            send_sem=r_send.at[step],
            recv_sem=r_recv.at[other],
            device_id={"tok": other},
            device_id_type=MESH,
        ).wait_recv()

    for step in range(1, count):
        send_part(step).start()
    in_buf[me] = out_buf[me]
    for step in range(1, count):
        take_part(step)
    for n in range(half):
        summed = in_buf[0, n].astype(jnp.float32)
        for i in range(1, count):
            summed += in_buf[i, n].astype(jnp.float32)
        all_buf[me, feat * half + n] = summed.astype(jnp.bfloat16)
    own = all_buf.at[me, pl.ds(feat * half, half)]
    across = pltpu.make_async_remote_copy(
        src_ref=own, dst_ref=own, send_sem=p_send, recv_sem=p_recv,
        device_id={"feat": 1 - feat}, device_id_type=MESH,
    )
    across.start()
    across.wait()
    spread(all_buf, m_send, m_recv, None)
    for step in range(1, count):
        send_part(step).wait_send()
    for i in range(count):
        m_ref[:, pl.ds(i * rows, rows), :] = all_buf[i]


def reduced(activations, down_rows, target):
    count = Z * Y * CORES
    tokens, features = activations.shape
    share = down_rows.shape[0]
    blocks = len(pairs(Z))
    half, rows = blocks // 2, BLOCK // count
    dma = pltpu.SemaphoreType.DMA
    bf16 = jnp.bfloat16
    whole = pl.BlockSpec(memory_space=pltpu.VMEM)
    return pl.pallas_call(
        reduce_kernel,
        out_shape=(
            jax.ShapeDtypeStruct((Z, tokens, BLOCK), bf16),
            jax.ShapeDtypeStruct((blocks, BLOCK, BLOCK), bf16),
        ),
        in_specs=[pl.BlockSpec(memory_space=pl.ANY)] * 2 + [whole],
        out_specs=(whole, whole),
        scratch_shapes=[
            pltpu.VMEM((tokens, features), bf16),
            pltpu.VMEM((count, share, features), bf16),
            pltpu.VMEM((tokens, BLOCK), jnp.float32),
            pltpu.VMEM((Z, tokens, BLOCK), bf16),
            pltpu.VMEM((Z, tokens, BLOCK), bf16),
            pltpu.VMEM((count, half, rows, BLOCK), bf16),
            pltpu.VMEM((count, half, rows, BLOCK), bf16),
            pltpu.VMEM((count, blocks, rows, BLOCK), bf16),
            dma, dma, dma((4, count)), dma((count,)), dma((Z,)), dma((Z,)),
            dma((count,)), dma((count,)), dma, dma, dma((4, count)), dma((count,)),
        ],
        compiler_params=pltpu.CompilerParams(
            collective_id=0, has_side_effects=True, vmem_limit_bytes=56 * 2**20
        ),
        cost_estimate=pl.CostEstimate(
            flops=2 * tokens * features * share * count, bytes_accessed=2 * tokens * features, transcendentals=0
        ),
    )(activations, down_rows, target)


def solve_gram(matrix, right):
    lower = jnp.linalg.cholesky(matrix)
    middle = lax.linalg.triangular_solve(lower, right, left_side=True, lower=True)
    return lax.linalg.triangular_solve(lower, middle, left_side=True, lower=True, transpose_a=True)


def wide_dot(a, b, dims):
    return lax.dot_general(a, b, (dims, ((), ())), preferred_element_type=jnp.float32)


def on_block(activations, down_proj, precond, target):
    feat_index = lax.axis_index("feat")
    joined, sums = reduced(activations, down_proj.T, target)
    blocks = dict(zip(pairs(Z), sums))
    normal = jnp.concatenate(
        [
            jnp.concatenate([blocks[i, j] if i <= j else blocks[j, i].T for j in range(Z)], axis=1)
            for i in range(Z)
        ],
        axis=0,
    )
    back = jnp.concatenate([blocks[i, None] for i in range(Z)], axis=0).astype(jnp.float32)

    def gradient(current):
        descent = wide_dot(precond, current.astype(jnp.bfloat16), ((0,), (0,)))
        return descent, jnp.dot(descent.T, descent, precision=precise)

    descent, gram_now = gradient(back)
    direction = descent
    answer = jnp.zeros(back.shape, jnp.float32)
    for iteration in range(ITERS):
        lift = wide_dot(precond, direction.astype(jnp.bfloat16), ((1,), (0,)))
        rounded = lift.astype(jnp.bfloat16)
        pushed = wide_dot(normal, rounded, ((1,), (0,)))
        curvature = jnp.dot(rounded.astype(jnp.float32).T, pushed, precision=precise)
        curvature = 0.5 * (curvature + curvature.T)
        step_size = solve_gram(curvature, gram_now)
        answer = answer + jnp.dot(lift, step_size, precision=precise)
        if iteration + 1 < ITERS:
            back = back - jnp.dot(pushed, step_size, precision=precise)
            descent, gram_next = gradient(back)
            mixing = solve_gram(gram_now, gram_next)
            direction = descent + jnp.dot(direction, mixing, precision=precise)
            gram_now = gram_next
    rounded = answer.astype(jnp.bfloat16).reshape(Z, BLOCK, -1)
    fitted = sum(wide_dot(joined[i], rounded[i], ((1,), (0,))) for i in range(Z))
    share = answer.shape[0] // lax.axis_size("feat")
    return (
        lax.dynamic_slice_in_dim(answer, feat_index * share, share, 0),
        target.astype(jnp.float32) - fitted,
    )


def on_device(activations, down_proj, precond, target):
    feat_count = lax.axis_size("feat")
    feat_index = lax.axis_index("feat")
    share_rows = precond.shape[0] // feat_count
    partial_map = jnp.dot(
        activations,
        lax.all_gather(down_proj, "tok", axis=1, tiled=True),
        preferred_element_type=jnp.float32,
    )
    joined_share = lax.psum_scatter(partial_map, "feat", scatter_dimension=1, tiled=True).astype(
        jnp.bfloat16
    )
    row_block = lax.dynamic_slice_in_dim(precond, feat_index * share_rows, share_rows, 0)
    col_block = lax.dynamic_slice_in_dim(precond, feat_index * share_rows, share_rows, 1)

    def gradient(current):
        partial_back = lax.dot_general(
            joined_share,
            current.astype(jnp.bfloat16),
            (((0,), (0,)), ((), ())),
            preferred_element_type=jnp.float32,
        )
        summed = lax.psum(partial_back, "tok")
        gathered = lax.all_gather(summed.astype(jnp.bfloat16), "feat", axis=0, tiled=True)
        descent = lax.dot_general(
            col_block, gathered, (((0,), (0,)), ((), ())), preferred_element_type=jnp.float32
        )
        gram_matrix = lax.psum(jnp.dot(descent.T, descent, precision=precise), "feat")
        return (descent, gram_matrix)

    residual = target.astype(jnp.float32)
    descent, gram_now = gradient(residual)
    direction = descent
    solution = jnp.zeros((share_rows, target.shape[1]), jnp.float32)
    for iteration in range(ITERS):
        rounded_dir = lax.all_gather(direction.astype(jnp.bfloat16), "feat", axis=0, tiled=True)
        lift_rows = jnp.dot(row_block, rounded_dir, preferred_element_type=jnp.float32)
        partial_image = jnp.dot(
            joined_share, lift_rows.astype(jnp.bfloat16), preferred_element_type=jnp.float32
        )
        image_now = lax.psum(partial_image, "feat")
        curvature = lax.psum(jnp.dot(image_now.T, image_now, precision=precise), "tok")
        step_size = solve_gram(curvature, gram_now)
        solution = solution + jnp.dot(lift_rows, step_size, precision=precise)
        residual = residual - jnp.dot(image_now, step_size, precision=precise)
        if iteration + 1 < ITERS:
            descent, gram_next = gradient(residual)
            mixing = solve_gram(gram_now, gram_next)
            direction = descent + jnp.dot(direction, mixing, precision=precise)
            gram_now = gram_next
    return (solution, residual)


def solution(mesh):
    small = mesh.shape["tok"] == Z * Y * CORES and mesh.shape["feat"] == 2
    placed = (P("tok", "feat"), P("feat", "tok"), P(), P("tok", None))
    return jax.shard_map(
        on_block if small else on_device,
        mesh=mesh,
        in_specs=placed,
        out_specs=(P("feat", None), P("tok", None)),
        check_vma=False,
    )
```

```python
import functools

import jax
import jax.numpy as jnp
from jax import lax
from jax.experimental import pallas as pl
from jax.experimental.pallas import tpu as pltpu
from jax.sharding import PartitionSpec as P

ITERS = 2
Z, Y, CORES = 4, 2, 2
BLOCK = 256
DEPTH = 1024
MESH = pl.DeviceIdType.MESH
precise = lax.Precision.HIGHEST


def spread(buf, send, recv, on_slab):
    me = lax.axis_index("tok")
    z, y, c = me // (Y * CORES), (me // CORES) % Y, me % CORES

    def index(zz, yy, cc):
        return (zz * Y + yy) * CORES + cc

    targets = (me + Y * CORES, me - Y * CORES, index(z, 1 - y, c), index(z, y, 1 - c))

    def copy(i, way):
        return pltpu.make_async_remote_copy(
            src_ref=buf.at[i],
            dst_ref=buf.at[i],
            send_sem=send.at[way, i],
            recv_sem=recv.at[i],
            device_id={"tok": targets[way]},
            device_id_type=MESH,
        )

    def along(distance, visit):
        for sign in (1, -1) if distance else (1,):
            zz = z + sign * distance

            @pl.when((zz >= 0) & (zz < Z))
            def _():
                visit(zz, sign)

    def onward(i, zz, sign, act):
        if sign != 1 or zz is z:

            @pl.when(z < Z - 1)
            def _():
                act(copy(i, 0))

        if sign == 1:

            @pl.when(z > 0)
            def _():
                act(copy(i, 1))

        act(copy(i, 2))
        act(copy(i, 3))

    onward(me, z, 1, lambda k: k.start())
    for stage in range(Z):

        def line(zz, sign):
            i = index(zz, y, c)
            copy(i, 2).wait_recv()
            onward(i, zz, sign, lambda k: k.start())

        def side(zz, sign):
            i = index(zz, 1 - y, c)
            copy(i, 2).wait_recv()
            copy(i, 3).start()

        def slab(zz, sign):
            copy(index(zz, y, 1 - c), 3).wait_recv()
            copy(index(zz, 1 - y, 1 - c), 3).wait_recv()
            if on_slab is not None:
                on_slab(zz)

        if stage + 1 < Z:
            along(stage + 1, line)
        along(stage, side)
        along(stage, slab)

    onward(me, z, 1, lambda k: k.wait_send())
    for stage in range(Z):
        if stage:
            along(stage, lambda zz, sign: onward(index(zz, y, c), zz, sign, lambda k: k.wait_send()))
        along(stage, lambda zz, sign: copy(index(zz, 1 - y, c), 3).wait_send())


def pairs(slabs):
    upper = [(i, j) for i in range(slabs) for j in range(i, slabs)]
    return upper + [(i, None) for i in range(slabs)]


def reduce_kernel(
    a_ref, d_ref, t_ref, j_ref, m_ref,
    a_buf, d_buf, total, mine, theirs, out_buf, in_buf, all_buf,
    a_sem, d_sem, d_send, d_recv, x_send, x_recv, r_send, r_recv, p_send, p_recv, m_send, m_recv,
):
    me, feat = lax.axis_index("tok"), lax.axis_index("feat")
    count = Z * Y * CORES
    group = Y * CORES

    load_a = pltpu.make_async_copy(a_ref, a_buf, a_sem)
    load_d = pltpu.make_async_copy(d_ref, d_buf.at[me], d_sem)
    load_d.start()
    load_a.start()

    barrier = pltpu.get_barrier_semaphore()
    for step in range(1, count):
        pl.semaphore_signal(
            barrier, inc=1, device_id={"tok": lax.rem(me + step, count)}, device_id_type=MESH
        )
    pl.semaphore_signal(barrier, inc=1, device_id={"feat": 1 - feat}, device_id_type=MESH)
    pl.semaphore_wait(barrier, count)
    load_d.wait()

    def swap(slab):
        return pltpu.make_async_remote_copy(
            src_ref=mine.at[slab],
            dst_ref=theirs.at[slab],
            send_sem=x_send.at[slab],
            recv_sem=x_recv.at[slab],
            device_id={"feat": 1 - feat},
            device_id_type=MESH,
        )

    def project(slab):
        total[...] = jnp.zeros_like(total)

        def part(k, carry):
            columns = pl.ds(pl.multiple_of(k * DEPTH, DEPTH), DEPTH)
            weights = d_buf[pl.ds(slab * group, group), :, columns].reshape(BLOCK, DEPTH)
            total[...] += lax.dot_general(
                a_buf[:, columns], weights, (((1,), (1,)), ((), ())), preferred_element_type=jnp.float32
            )
            return carry

        lax.fori_loop(0, a_buf.shape[1] // DEPTH, part, 0)
        mine[slab] = total[...].astype(jnp.bfloat16)
        swap(slab).start()

    load_a.wait()
    spread(d_buf, d_send, d_recv, project)
    for slab in range(Z):
        swap(slab).wait()
        j_ref[slab] = (mine[slab].astype(jnp.float32) + theirs[slab].astype(jnp.float32)).astype(
            jnp.bfloat16
        )

    blocks = pairs(Z)
    half = len(blocks) // 2
    rows = BLOCK // count
    for owner in range(2):

        @pl.when(feat == owner)
        def _():
            for n, (i, j) in enumerate(blocks[owner * half : (owner + 1) * half]):
                product = lax.dot_general(
                    t_ref[...] if j is None else j_ref[i],
                    j_ref[i if j is None else j],
                    (((0,), (0,)), ((), ())),
                    preferred_element_type=jnp.float32,
                )
                out_buf[:, n] = product.astype(jnp.bfloat16).reshape(count, rows, BLOCK)

    def send_part(step):
        other = lax.rem(me + step, count)
        return pltpu.make_async_remote_copy(
            src_ref=out_buf.at[other],
            dst_ref=in_buf.at[me],
            send_sem=r_send.at[step],
            recv_sem=r_recv.at[me],
            device_id={"tok": other},
            device_id_type=MESH,
        )

    def take_part(step):
        other = lax.rem(me + step, count)
        pltpu.make_async_remote_copy(
            src_ref=out_buf.at[other],
            dst_ref=in_buf.at[other],
            send_sem=r_send.at[step],
            recv_sem=r_recv.at[other],
            device_id={"tok": other},
            device_id_type=MESH,
        ).wait_recv()

    for step in range(1, count):
        send_part(step).start()
    in_buf[me] = out_buf[me]
    for step in range(1, count):
        take_part(step)
    for n in range(half):
        summed = in_buf[0, n].astype(jnp.float32)
        for i in range(1, count):
            summed += in_buf[i, n].astype(jnp.float32)
        all_buf[me, feat * half + n] = summed.astype(jnp.bfloat16)
    own = all_buf.at[me, pl.ds(feat * half, half)]
    across = pltpu.make_async_remote_copy(
        src_ref=own, dst_ref=own, send_sem=p_send, recv_sem=p_recv,
        device_id={"feat": 1 - feat}, device_id_type=MESH,
    )
    across.start()
    across.wait()
    spread(all_buf, m_send, m_recv, None)
    for step in range(1, count):
        send_part(step).wait_send()
    for i in range(count):
        m_ref[:, pl.ds(i * rows, rows), :] = all_buf[i]


def reduced(activations, down_rows, target):
    count = Z * Y * CORES
    tokens, features = activations.shape
    share = down_rows.shape[0]
    blocks = len(pairs(Z))
    half, rows = blocks // 2, BLOCK // count
    dma = pltpu.SemaphoreType.DMA
    bf16 = jnp.bfloat16
    whole = pl.BlockSpec(memory_space=pltpu.VMEM)
    return pl.pallas_call(
        reduce_kernel,
        out_shape=(
            jax.ShapeDtypeStruct((Z, tokens, BLOCK), bf16),
            jax.ShapeDtypeStruct((blocks, BLOCK, BLOCK), bf16),
        ),
        in_specs=[pl.BlockSpec(memory_space=pl.ANY)] * 2 + [whole],
        out_specs=(whole, whole),
        scratch_shapes=[
            pltpu.VMEM((tokens, features), bf16),
            pltpu.VMEM((count, share, features), bf16),
            pltpu.VMEM((tokens, BLOCK), jnp.float32),
            pltpu.VMEM((Z, tokens, BLOCK), bf16),
            pltpu.VMEM((Z, tokens, BLOCK), bf16),
            pltpu.VMEM((count, half, rows, BLOCK), bf16),
            pltpu.VMEM((count, half, rows, BLOCK), bf16),
            pltpu.VMEM((count, blocks, rows, BLOCK), bf16),
            dma, dma, dma((4, count)), dma((count,)), dma((Z,)), dma((Z,)),
            dma((count,)), dma((count,)), dma, dma, dma((4, count)), dma((count,)),
        ],
        compiler_params=pltpu.CompilerParams(
            collective_id=0, has_side_effects=True, vmem_limit_bytes=56 * 2**20
        ),
        cost_estimate=pl.CostEstimate(
            flops=2 * tokens * features * share * count, bytes_accessed=2 * tokens * features, transcendentals=0
        ),
    )(activations, down_rows, target)


def dot(a, b, dims, precision=None):
    return lax.dot_general(
        a, b, (dims, ((), ())), precision=precision, preferred_element_type=jnp.float32
    )


PLAIN, ACROSS = ((1,), (0,)), ((1,), (1,))
HALF = BLOCK // 2


def invert(work, count):
    height = 8
    lane = lax.broadcasted_iota(jnp.int32, (1, HALF), 1)
    row = lax.broadcasted_iota(jnp.int32, (height, HALF), 0)
    tiles = [
        [work[n, pl.ds(i * height, height), :] for i in range(HALF // height)] for n in range(count)
    ]
    for p in range(0, HALF, 2):
        at, r = p // height, p % height
        first, second = lane == p, lane == p + 1
        for n in range(count):
            old = tiles[n]
            shape = (height, HALF)
            left = [jnp.broadcast_to(t[:, p : p + 1], shape) for t in old]
            right = [jnp.broadcast_to(t[:, p + 1 : p + 2], shape) for t in old]
            a00, a10 = left[at][r : r + 1], left[at][r + 1 : r + 2]
            a01, a11 = right[at][r : r + 1], right[at][r + 1 : r + 2]
            over = 1.0 / a00
            s, t = a01 * over, a10 * over
            low = 1.0 / (a11 - a10 * s)
            top0 = jnp.where(first, 1.0, jnp.where(second, 0.0, old[at][r : r + 1]))
            top1 = jnp.where(first, 0.0, jnp.where(second, 1.0, old[at][r + 1 : r + 2]))
            w1 = low * (top1 - t * top0)
            w0 = over * top0 - s * w1
            left[at] = jnp.where(row == r, -1.0, jnp.where(row == r + 1, 0.0, left[at]))
            right[at] = jnp.where(row == r, 0.0, jnp.where(row == r + 1, -1.0, right[at]))
            both = first | second
            new = []
            for i, tile in enumerate(old):
                kept = jnp.where(both, 0.0, tile)
                if i == at:
                    kept = jnp.where((row == r) | (row == r + 1), 0.0, kept)
                new.append(kept - left[i] * w0 - right[i] * w1)
            tiles[n] = new
    for n in range(count):
        for i, tile in enumerate(tiles[n]):
            work[n, pl.ds(i * height, height), :] = tile


def iterate_kernel(
    m_ref, p_ref, j_ref, t_ref, answer_ref, residual_ref,
    normal, back, direction, lift, pushed, answer, gram, systems, work, inverse, upper,
):
    feat = lax.axis_index("feat")
    blocks = pairs(Z)
    for n, (i, j) in enumerate(blocks):
        rows = slice(i * BLOCK, (i + 1) * BLOCK)
        if j is None:
            back[:, rows] = m_ref[n].astype(jnp.float32)
            continue
        columns = slice(j * BLOCK, (j + 1) * BLOCK)
        normal[rows, columns] = m_ref[n]
        if i != j:
            normal[columns, rows] = m_ref[n].T

    def gradient():
        descent = dot(back[...].astype(jnp.bfloat16), p_ref[...], PLAIN)
        return descent, dot(descent, descent, ACROSS, precise)

    def factor():
        def step(block, carry):
            for n in range(2):

                @pl.when(block == 0)
                def _():
                    work[n] = systems[n, :HALF, :HALF]

                @pl.when(block == 1)
                def _():
                    upper[n] = dot(inverse[0, n], systems[n, :HALF, HALF:], PLAIN, precise)
                    work[n] = systems[n, HALF:, HALF:] - dot(
                        systems[n, HALF:, :HALF], upper[n], PLAIN, precise
                    )

            invert(work, 2)
            for n in range(2):
                inverse[block, n] = work[n]
            return carry

        lax.fori_loop(0, 2, step, 0)

    def solve(n, right):
        begun = dot(inverse[0, n], right[:HALF], PLAIN, precise)
        rest = right[HALF:] - dot(systems[n, HALF:, :HALF], begun, PLAIN, precise)
        lower = dot(inverse[1, n], rest, PLAIN, precise)
        return jnp.concatenate([begun - dot(upper[n], lower, PLAIN, precise), lower], axis=0)

    descent, first = gradient()
    direction[...] = descent
    gram[...] = first
    answer[...] = jnp.zeros_like(answer)

    def iteration(index, carry):
        lift[...] = dot(direction[...].astype(jnp.bfloat16), p_ref[...], ACROSS)
        rounded = lift[...].astype(jnp.bfloat16)
        pushed[...] = dot(rounded, normal[...], PLAIN)
        systems[0] = dot(rounded.astype(jnp.float32), pushed[...], ACROSS, precise)
        systems[1] = gram[...]
        factor()
        step_size = solve(0, gram[...]).T
        answer[...] += dot(step_size, lift[...], PLAIN, precise)

        @pl.when(index + 1 < ITERS)
        def _():
            back[...] -= dot(step_size, pushed[...], PLAIN, precise)
            descent, following = gradient()
            mixing = solve(1, following).T
            direction[...] = descent + dot(mixing, direction[...], PLAIN, precise)
            gram[...] = following

        return carry

    lax.fori_loop(0, ITERS, iteration, 0)
    fitted = jnp.zeros(residual_ref.shape, jnp.float32)
    for i in range(Z):
        fitted += dot(j_ref[i], answer[:, i * BLOCK : (i + 1) * BLOCK].astype(jnp.bfloat16), ACROSS)
    residual_ref[...] = t_ref[...].astype(jnp.float32) - fitted
    share = answer_ref.shape[0]
    answer_ref[...] = answer[:, pl.ds(pl.multiple_of(feat * share, share), share)].T


def on_block(activations, down_proj, precond, target):
    joined, sums = reduced(activations, down_proj.T, target)
    rank, wanted = precond.shape[0], target.shape[1]
    f32 = jnp.float32
    whole = pl.BlockSpec(memory_space=pltpu.VMEM)
    wide, square, small = (wanted, rank), (wanted, wanted), (2, HALF, HALF)
    return pl.pallas_call(
        iterate_kernel,
        out_shape=(
            jax.ShapeDtypeStruct((rank // lax.axis_size("feat"), wanted), f32),
            jax.ShapeDtypeStruct(target.shape, f32),
        ),
        in_specs=[whole] * 4,
        out_specs=(whole, whole),
        scratch_shapes=[
            pltpu.VMEM((rank, rank), jnp.bfloat16),
            pltpu.VMEM(wide, f32),
            pltpu.VMEM(wide, f32),
            pltpu.VMEM(wide, f32),
            pltpu.VMEM(wide, f32),
            pltpu.VMEM(wide, f32),
            pltpu.VMEM(square, f32),
            pltpu.VMEM((2,) + square, f32),
            pltpu.VMEM(small, f32),
            pltpu.VMEM((2,) + small, f32),
            pltpu.VMEM(small, f32),
        ],
        compiler_params=pltpu.CompilerParams(vmem_limit_bytes=48 * 2**20),
    )(sums, precond, joined, target)


def solve_gram(matrix, right):
    lower = jnp.linalg.cholesky(matrix)
    middle = lax.linalg.triangular_solve(lower, right, left_side=True, lower=True)
    return lax.linalg.triangular_solve(lower, middle, left_side=True, lower=True, transpose_a=True)


def on_device(activations, down_proj, precond, target):
    feat_count = lax.axis_size("feat")
    feat_index = lax.axis_index("feat")
    share_rows = precond.shape[0] // feat_count
    partial_map = jnp.dot(
        activations,
        lax.all_gather(down_proj, "tok", axis=1, tiled=True),
        preferred_element_type=jnp.float32,
    )
    joined_share = lax.psum_scatter(partial_map, "feat", scatter_dimension=1, tiled=True).astype(
        jnp.bfloat16
    )
    row_block = lax.dynamic_slice_in_dim(precond, feat_index * share_rows, share_rows, 0)
    col_block = lax.dynamic_slice_in_dim(precond, feat_index * share_rows, share_rows, 1)

    def gradient(current):
        partial_back = lax.dot_general(
            joined_share,
            current.astype(jnp.bfloat16),
            (((0,), (0,)), ((), ())),
            preferred_element_type=jnp.float32,
        )
        summed = lax.psum(partial_back, "tok")
        gathered = lax.all_gather(summed.astype(jnp.bfloat16), "feat", axis=0, tiled=True)
        descent = lax.dot_general(
            col_block, gathered, (((0,), (0,)), ((), ())), preferred_element_type=jnp.float32
        )
        gram_matrix = lax.psum(jnp.dot(descent.T, descent, precision=precise), "feat")
        return (descent, gram_matrix)

    residual = target.astype(jnp.float32)
    descent, gram_now = gradient(residual)
    direction = descent
    solution = jnp.zeros((share_rows, target.shape[1]), jnp.float32)
    for iteration in range(ITERS):
        rounded_dir = lax.all_gather(direction.astype(jnp.bfloat16), "feat", axis=0, tiled=True)
        lift_rows = jnp.dot(row_block, rounded_dir, preferred_element_type=jnp.float32)
        partial_image = jnp.dot(
            joined_share, lift_rows.astype(jnp.bfloat16), preferred_element_type=jnp.float32
        )
        image_now = lax.psum(partial_image, "feat")
        curvature = lax.psum(jnp.dot(image_now.T, image_now, precision=precise), "tok")
        step_size = solve_gram(curvature, gram_now)
        solution = solution + jnp.dot(lift_rows, step_size, precision=precise)
        residual = residual - jnp.dot(image_now, step_size, precision=precise)
        if iteration + 1 < ITERS:
            descent, gram_next = gradient(residual)
            mixing = solve_gram(gram_now, gram_next)
            direction = descent + jnp.dot(direction, mixing, precision=precise)
            gram_now = gram_next
    return (solution, residual)


def solution(mesh):
    small = mesh.shape["tok"] == Z * Y * CORES and mesh.shape["feat"] == 2
    placed = (P("tok", "feat"), P("feat", "tok"), P(), P("tok", None))
    return jax.shard_map(
        on_block if small else on_device,
        mesh=mesh,
        in_specs=placed,
        out_specs=(P("feat", None), P("tok", None)),
        check_vma=False,
    )
```

```python
import functools

import jax
import jax.numpy as jnp
from jax import lax
from jax.experimental import pallas as pl
from jax.experimental.pallas import tpu as pltpu
from jax.sharding import PartitionSpec as P

ITERS = 2
Z, Y, CORES = 4, 2, 2
BLOCK = 256
DEPTH = 1024
MESH = pl.DeviceIdType.MESH
precise = lax.Precision.HIGHEST


def spread(views, side_first, send, recv, on_slab):
    me = lax.axis_index("tok")
    z, y, c = me // (Y * CORES), (me // CORES) % Y, me % CORES
    parts = range(len(views))

    def index(zz, yy, cc):
        return (zz * Y + yy) * CORES + cc

    targets = (me + Y * CORES, me - Y * CORES, index(z, 1 - y, c), index(z, y, 1 - c))

    def copy(n, i, way):
        return pltpu.make_async_remote_copy(
            src_ref=views[n](i),
            dst_ref=views[n](i),
            send_sem=send.at[n, way, i],
            recv_sem=recv.at[n, i],
            device_id={"tok": targets[way]},
            device_id_type=MESH,
        )

    def along(distance, visit):
        for sign in (1, -1) if distance else (0,):
            zz = z + sign * distance

            @pl.when((zz >= 0) & (zz < Z))
            def _():
                visit(zz, sign)

    def onward(act, n, i, sign, side):
        if side:
            act(copy(n, i, 2))
        if sign is not None and sign <= 0:

            @pl.when(z < Z - 1)
            def _():
                act(copy(n, i, 0))

        if sign is not None and sign >= 0:

            @pl.when(z > 0)
            def _():
                act(copy(n, i, 1))

        act(copy(n, i, 3))

    def begin(act):
        for n in parts[::-1]:
            onward(act, n, me, 0, True)

    def lines(zz, sign, act, arrive):
        for n in parts:
            for yy in (y, 1 - y) if side_first[n] else (y,):
                i = index(zz, yy, c)
                if arrive is not None:
                    arrive(copy(n, i, 3))
                onward(act, n, i, sign, not side_first[n])

    def sides(zz, act, arrive, first):
        for n in parts:
            if side_first[n] == first:
                i = index(zz, 1 - y, c)
                if arrive is not None:
                    arrive(copy(n, i, 3))
                onward(act, n, i, 0 if first else None, False)

    def start(copied):
        copied.start()

    def arrived(copied):
        copied.wait_recv()

    def sent(copied):
        copied.wait_send()

    def slab(zz, sign):
        for n in parts:
            for yy in (y, 1 - y):
                arrived(copy(n, index(zz, yy, 1 - c), 3))
        if on_slab is not None:
            on_slab(zz)

    begin(start)
    sides(z, start, arrived, True)
    for stage in range(Z):
        if stage + 1 < Z:
            along(stage + 1, lambda zz, sign: lines(zz, sign, start, arrived))
        along(stage, lambda zz, sign: sides(zz, start, arrived, False))
        along(stage, slab)

    begin(sent)
    sides(z, sent, None, True)
    for stage in range(Z):
        if stage + 1 < Z:
            along(stage + 1, lambda zz, sign: lines(zz, sign, sent, None))
        along(stage, lambda zz, sign: sides(zz, sent, None, False))


def pairs(slabs):
    upper = [(i, j) for i in range(slabs) for j in range(i, slabs)]
    return upper + [(i, None) for i in range(slabs)]


def reduce_kernel(
    a_ref, d_ref, t_ref, j_ref, m_ref,
    a_buf, d_buf, total, mine, theirs, out_buf, core_buf, pair_buf, in_buf, all_buf,
    a_sem, d_sem, d_send, d_recv, x_send, x_recv, c_send, c_recv, r_send, r_recv, p_send, p_recv, m_send, m_recv,
):
    me, feat = lax.axis_index("tok"), lax.axis_index("feat")
    count = Z * Y * CORES
    group = Y * CORES

    load_a = pltpu.make_async_copy(a_ref, a_buf, a_sem)
    load_d = pltpu.make_async_copy(d_ref, d_buf.at[me], d_sem)
    load_d.start()
    load_a.start()

    barrier = pltpu.get_barrier_semaphore()
    for step in range(1, count):
        pl.semaphore_signal(
            barrier, inc=1, device_id={"tok": lax.rem(me + step, count)}, device_id_type=MESH
        )
    pl.semaphore_signal(barrier, inc=1, device_id={"feat": 1 - feat}, device_id_type=MESH)
    pl.semaphore_wait(barrier, count)
    load_d.wait()

    def swap(slab):
        return pltpu.make_async_remote_copy(
            src_ref=mine.at[slab],
            dst_ref=theirs.at[slab],
            send_sem=x_send.at[slab],
            recv_sem=x_recv.at[slab],
            device_id={"feat": 1 - feat},
            device_id_type=MESH,
        )

    def project(slab):
        total[...] = jnp.zeros_like(total)

        def part(k, carry):
            columns = pl.ds(pl.multiple_of(k * DEPTH, DEPTH), DEPTH)
            weights = d_buf[pl.ds(slab * group, group), :, columns].reshape(BLOCK, DEPTH)
            total[...] += lax.dot_general(
                a_buf[:, columns], weights, (((1,), (1,)), ((), ())), preferred_element_type=jnp.float32
            )
            return carry

        lax.fori_loop(0, a_buf.shape[1] // DEPTH, part, 0)
        mine[slab] = total[...].astype(jnp.bfloat16)
        swap(slab).start()

    load_a.wait()
    eighth = d_buf.shape[2] // 8
    views = [
        lambda i, low=low, size=size: d_buf.at[i, :, pl.ds(low * eighth, size * eighth)]
        for low, size in ((0, 3), (3, 4), (7, 1))
    ]
    spread(views, (False, False, True), d_send, d_recv, project)
    for slab in range(Z):
        swap(slab).wait()
        j_ref[slab] = (mine[slab].astype(jnp.float32) + theirs[slab].astype(jnp.float32)).astype(
            jnp.bfloat16
        )

    blocks = pairs(Z)
    half = len(blocks) // 2
    rows, chips = BLOCK // count, Z * Y
    for owner in range(2):

        @pl.when(feat == owner)
        def _():
            for n, (i, j) in enumerate(blocks[owner * half : (owner + 1) * half]):
                product = lax.dot_general(
                    t_ref[...] if j is None else j_ref[i],
                    j_ref[i if j is None else j],
                    (((0,), (0,)), ((), ())),
                    preferred_element_type=jnp.float32,
                )
                out_buf[:, :, n] = product.astype(jnp.bfloat16).reshape(CORES, chips, rows, BLOCK)

    chip, core = me // CORES, me % CORES
    between = pltpu.make_async_remote_copy(
        src_ref=out_buf.at[1 - core],
        dst_ref=core_buf,
        send_sem=c_send,
        recv_sem=c_recv,
        device_id={"tok": chip * CORES + 1 - core},
        device_id_type=MESH,
    )
    between.start()
    between.wait()
    for i in range(chips):
        pair_buf[i] = (out_buf[core, i].astype(jnp.float32) + core_buf[i].astype(jnp.float32)).astype(
            jnp.bfloat16
        )

    def part(step, slot, sem):
        other = lax.rem(chip + step, chips)
        return pltpu.make_async_remote_copy(
            src_ref=pair_buf.at[other],
            dst_ref=in_buf.at[slot],
            send_sem=r_send.at[step],
            recv_sem=r_recv.at[sem],
            device_id={"tok": other * CORES + core},
            device_id_type=MESH,
        )

    for step in range(1, chips):
        part(step, chip, chip).start()
    in_buf[chip] = pair_buf[chip]
    for step in range(1, chips):
        other = lax.rem(chip + step, chips)
        part(step, other, other).wait_recv()
    for n in range(half):
        summed = in_buf[0, n].astype(jnp.float32)
        for i in range(1, chips):
            summed += in_buf[i, n].astype(jnp.float32)
        all_buf[me, feat * half + n] = summed.astype(jnp.bfloat16)
    own = all_buf.at[me, pl.ds(feat * half, half)]
    across = pltpu.make_async_remote_copy(
        src_ref=own, dst_ref=own, send_sem=p_send, recv_sem=p_recv,
        device_id={"feat": 1 - feat}, device_id_type=MESH,
    )
    across.start()
    across.wait()
    spread([lambda i: all_buf.at[i]], (False,), m_send, m_recv, None)
    for step in range(1, chips):
        part(step, chip, chip).wait_send()
    for i in range(count):
        place = (i % CORES) * chips + i // CORES
        m_ref[:, pl.ds(place * rows, rows), :] = all_buf[i]


def reduced(activations, down_rows, target):
    count = Z * Y * CORES
    tokens, features = activations.shape
    share = down_rows.shape[0]
    blocks = len(pairs(Z))
    half, rows, chips = blocks // 2, BLOCK // count, Z * Y
    dma = pltpu.SemaphoreType.DMA
    bf16 = jnp.bfloat16
    whole = pl.BlockSpec(memory_space=pltpu.VMEM)
    return pl.pallas_call(
        reduce_kernel,
        out_shape=(
            jax.ShapeDtypeStruct((Z, tokens, BLOCK), bf16),
            jax.ShapeDtypeStruct((blocks, BLOCK, BLOCK), bf16),
        ),
        in_specs=[pl.BlockSpec(memory_space=pl.ANY)] * 2 + [whole],
        out_specs=(whole, whole),
        scratch_shapes=[
            pltpu.VMEM((tokens, features), bf16),
            pltpu.VMEM((count, share, features), bf16),
            pltpu.VMEM((tokens, BLOCK), jnp.float32),
            pltpu.VMEM((Z, tokens, BLOCK), bf16),
            pltpu.VMEM((Z, tokens, BLOCK), bf16),
            pltpu.VMEM((CORES, chips, half, rows, BLOCK), bf16),
            pltpu.VMEM((chips, half, rows, BLOCK), bf16),
            pltpu.VMEM((chips, half, rows, BLOCK), bf16),
            pltpu.VMEM((chips, half, rows, BLOCK), bf16),
            pltpu.VMEM((count, blocks, rows, BLOCK), bf16),
            dma, dma, dma((3, 4, count)), dma((3, count)), dma((Z,)), dma((Z,)), dma, dma,
            dma((chips,)), dma((chips,)), dma, dma, dma((1, 4, count)), dma((1, count)),
        ],
        compiler_params=pltpu.CompilerParams(
            collective_id=0, has_side_effects=True, vmem_limit_bytes=56 * 2**20
        ),
        cost_estimate=pl.CostEstimate(
            flops=2 * tokens * features * share * count, bytes_accessed=2 * tokens * features, transcendentals=0
        ),
    )(activations, down_rows, target)


def dot(a, b, dims, precision=None):
    return lax.dot_general(
        a, b, (dims, ((), ())), precision=precision, preferred_element_type=jnp.float32
    )


PLAIN, ACROSS = ((1,), (0,)), ((1,), (1,))
HALF = BLOCK // 2


def invert(work, scaled, count):
    height = 8
    lane = lax.broadcasted_iota(jnp.int32, (1, HALF), 1)
    row = lax.broadcasted_iota(jnp.int32, (height, HALF), 0)
    shape = (height, HALF)
    tiles = [
        [work[n, pl.ds(i * height, height), :] for i in range(HALF // height)] for n in range(count)
    ]
    for p in range(0, HALF, 2):
        at, r = p // height, p % height
        first, second, done = lane == p, lane == p + 1, lane <= p + 1
        both = first | second
        for n in range(count):
            old = tiles[n]
            left = {i: jnp.broadcast_to(old[i][:, p : p + 1], shape) for i in range(at, len(old))}
            right = {i: jnp.broadcast_to(old[i][:, p + 1 : p + 2], shape) for i in range(at, len(old))}
            a00, a10 = left[at][r : r + 1], left[at][r + 1 : r + 2]
            a01, a11 = right[at][r : r + 1], right[at][r + 1 : r + 2]
            over = 1.0 / a00
            s, t = a01 * over, a10 * over
            low = 1.0 / (a11 - a10 * s)
            top0 = jnp.where(first, 1.0, jnp.where(second, 0.0, old[at][r : r + 1]))
            top1 = jnp.where(first, 0.0, jnp.where(second, 1.0, old[at][r + 1 : r + 2]))
            w1 = low * (top1 - t * top0)
            w0 = over * top0 - s * w1
            work[n, p : p + 1, :] = jnp.where(done, top0, 0.0)
            work[n, p + 1 : p + 2, :] = jnp.where(done, top1, 0.0)
            scaled[n, p : p + 1, :] = jnp.where(done, w0, 0.0)
            scaled[n, p + 1 : p + 2, :] = jnp.where(done, w1, 0.0)
            new = list(old)
            for i in range(at, len(old)):
                if i == at and r + 2 == height:
                    continue
                changed = jnp.where(both, 0.0, old[i]) - left[i] * w0 - right[i] * w1
                new[i] = jnp.where(row > r + 1, changed, old[i]) if i == at else changed
            tiles[n] = new
    for n in range(count):
        work[n] = dot(work[n], scaled[n], ((0,), (0,)), precise)


def iterate_kernel(
    m_ref, p_ref, j_ref, t_ref, answer_ref, residual_ref,
    normal, back, direction, lift, pushed, answer, gram, systems, work, scaled, inverse, upper,
):
    feat = lax.axis_index("feat")
    blocks = pairs(Z)
    for n, (i, j) in enumerate(blocks):
        rows = slice(i * BLOCK, (i + 1) * BLOCK)
        if j is None:
            back[:, rows] = m_ref[n].astype(jnp.float32)
            continue
        columns = slice(j * BLOCK, (j + 1) * BLOCK)
        normal[rows, columns] = m_ref[n]
        if i != j:
            normal[columns, rows] = m_ref[n].T

    def gradient():
        descent = dot(back[...].astype(jnp.bfloat16), p_ref[...], PLAIN)
        return descent, dot(descent, descent, ACROSS, precise)

    def factor(count):
        def step(block, carry):
            for n in range(count):

                @pl.when(block == 0)
                def _():
                    work[n] = systems[n, :HALF, :HALF]

                @pl.when(block == 1)
                def _():
                    upper[n] = dot(inverse[0, n], systems[n, :HALF, HALF:], PLAIN, precise)
                    work[n] = systems[n, HALF:, HALF:] - dot(
                        systems[n, HALF:, :HALF], upper[n], PLAIN, precise
                    )

            invert(work, scaled, count)
            for n in range(count):
                inverse[block, n] = work[n]
            return carry

        lax.fori_loop(0, 2, step, 0)

    def solve(n, right):
        begun = dot(inverse[0, n], right[:HALF], PLAIN, precise)
        rest = right[HALF:] - dot(systems[n, HALF:, :HALF], begun, PLAIN, precise)
        lower = dot(inverse[1, n], rest, PLAIN, precise)
        return jnp.concatenate([begun - dot(upper[n], lower, PLAIN, precise), lower], axis=0)

    descent, first = gradient()
    direction[...] = descent
    gram[...] = first
    answer[...] = jnp.zeros_like(answer)

    for index in range(ITERS):
        last = index + 1 == ITERS
        lift[...] = dot(direction[...].astype(jnp.bfloat16), p_ref[...], ACROSS)
        rounded = lift[...].astype(jnp.bfloat16)
        pushed[...] = dot(rounded, normal[...], PLAIN)
        systems[0] = dot(rounded.astype(jnp.float32), pushed[...], ACROSS, precise)
        systems[1] = gram[...]
        factor(1 if last else 2)
        step_size = solve(0, gram[...]).T
        answer[...] += dot(step_size, lift[...], PLAIN, precise)
        if not last:
            back[...] -= dot(step_size, pushed[...], PLAIN, precise)
            descent, following = gradient()
            mixing = solve(1, following).T
            direction[...] = descent + dot(mixing, direction[...], PLAIN, precise)
            gram[...] = following

    fitted = jnp.zeros(residual_ref.shape, jnp.float32)
    for i in range(Z):
        fitted += dot(j_ref[i], answer[:, i * BLOCK : (i + 1) * BLOCK].astype(jnp.bfloat16), ACROSS)
    residual_ref[...] = t_ref[...].astype(jnp.float32) - fitted
    share = answer_ref.shape[0]
    answer_ref[...] = answer[:, pl.ds(pl.multiple_of(feat * share, share), share)].T


def on_block(activations, down_proj, precond, target):
    joined, sums = reduced(activations, down_proj.T, target)
    rank, wanted = precond.shape[0], target.shape[1]
    f32 = jnp.float32
    whole = pl.BlockSpec(memory_space=pltpu.VMEM)
    wide, square, small = (wanted, rank), (wanted, wanted), (2, HALF, HALF)
    return pl.pallas_call(
        iterate_kernel,
        out_shape=(
            jax.ShapeDtypeStruct((rank // lax.axis_size("feat"), wanted), f32),
            jax.ShapeDtypeStruct(target.shape, f32),
        ),
        in_specs=[whole] * 4,
        out_specs=(whole, whole),
        scratch_shapes=[
            pltpu.VMEM((rank, rank), jnp.bfloat16),
            pltpu.VMEM(wide, f32),
            pltpu.VMEM(wide, f32),
            pltpu.VMEM(wide, f32),
            pltpu.VMEM(wide, f32),
            pltpu.VMEM(wide, f32),
            pltpu.VMEM(square, f32),
            pltpu.VMEM((2,) + square, f32),
            pltpu.VMEM(small, f32),
            pltpu.VMEM(small, f32),
            pltpu.VMEM((2,) + small, f32),
            pltpu.VMEM(small, f32),
        ],
        compiler_params=pltpu.CompilerParams(vmem_limit_bytes=48 * 2**20),
    )(sums, precond, joined, target)


def solve_gram(matrix, right):
    lower = jnp.linalg.cholesky(matrix)
    middle = lax.linalg.triangular_solve(lower, right, left_side=True, lower=True)
    return lax.linalg.triangular_solve(lower, middle, left_side=True, lower=True, transpose_a=True)


def on_device(activations, down_proj, precond, target):
    feat_count = lax.axis_size("feat")
    feat_index = lax.axis_index("feat")
    share_rows = precond.shape[0] // feat_count
    partial_map = jnp.dot(
        activations,
        lax.all_gather(down_proj, "tok", axis=1, tiled=True),
        preferred_element_type=jnp.float32,
    )
    joined_share = lax.psum_scatter(partial_map, "feat", scatter_dimension=1, tiled=True).astype(
        jnp.bfloat16
    )
    row_block = lax.dynamic_slice_in_dim(precond, feat_index * share_rows, share_rows, 0)
    col_block = lax.dynamic_slice_in_dim(precond, feat_index * share_rows, share_rows, 1)

    def gradient(current):
        partial_back = lax.dot_general(
            joined_share,
            current.astype(jnp.bfloat16),
            (((0,), (0,)), ((), ())),
            preferred_element_type=jnp.float32,
        )
        summed = lax.psum(partial_back, "tok")
        gathered = lax.all_gather(summed.astype(jnp.bfloat16), "feat", axis=0, tiled=True)
        descent = lax.dot_general(
            col_block, gathered, (((0,), (0,)), ((), ())), preferred_element_type=jnp.float32
        )
        gram_matrix = lax.psum(jnp.dot(descent.T, descent, precision=precise), "feat")
        return (descent, gram_matrix)

    residual = target.astype(jnp.float32)
    descent, gram_now = gradient(residual)
    direction = descent
    solution = jnp.zeros((share_rows, target.shape[1]), jnp.float32)
    for iteration in range(ITERS):
        rounded_dir = lax.all_gather(direction.astype(jnp.bfloat16), "feat", axis=0, tiled=True)
        lift_rows = jnp.dot(row_block, rounded_dir, preferred_element_type=jnp.float32)
        partial_image = jnp.dot(
            joined_share, lift_rows.astype(jnp.bfloat16), preferred_element_type=jnp.float32
        )
        image_now = lax.psum(partial_image, "feat")
        curvature = lax.psum(jnp.dot(image_now.T, image_now, precision=precise), "tok")
        step_size = solve_gram(curvature, gram_now)
        solution = solution + jnp.dot(lift_rows, step_size, precision=precise)
        residual = residual - jnp.dot(image_now, step_size, precision=precise)
        if iteration + 1 < ITERS:
            descent, gram_next = gradient(residual)
            mixing = solve_gram(gram_now, gram_next)
            direction = descent + jnp.dot(direction, mixing, precision=precise)
            gram_now = gram_next
    return (solution, residual)


def solution(mesh):
    small = mesh.shape["tok"] == Z * Y * CORES and mesh.shape["feat"] == 2
    placed = (P("tok", "feat"), P("feat", "tok"), P(), P("tok", None))
    return jax.shard_map(
        on_block if small else on_device,
        mesh=mesh,
        in_specs=placed,
        out_specs=(P("feat", None), P("tok", None)),
        check_vma=False,
    )
```

```python
import functools

import jax
import jax.numpy as jnp
from jax import lax
from jax.experimental import pallas as pl
from jax.experimental.pallas import tpu as pltpu
from jax.sharding import PartitionSpec as P

ITERS = 2
Z, Y, CORES = 4, 2, 2
BLOCK = 256
DEPTH = 1024
MESH = pl.DeviceIdType.MESH
precise = lax.Precision.HIGHEST


def spread(views, side_first, send, recv, on_slab):
    me = lax.axis_index("tok")
    z, y, c = me // (Y * CORES), (me // CORES) % Y, me % CORES
    parts = range(len(views))

    def index(zz, yy, cc):
        return (zz * Y + yy) * CORES + cc

    targets = (me + Y * CORES, me - Y * CORES, index(z, 1 - y, c), index(z, y, 1 - c))

    def copy(n, i, way):
        return pltpu.make_async_remote_copy(
            src_ref=views[n](i),
            dst_ref=views[n](i),
            send_sem=send.at[n, way, i],
            recv_sem=recv.at[n, i],
            device_id={"tok": targets[way]},
            device_id_type=MESH,
        )

    def along(distance, visit):
        for sign in (1, -1) if distance else (0,):
            zz = z + sign * distance

            @pl.when((zz >= 0) & (zz < Z))
            def _():
                visit(zz, sign)

    def onward(act, n, i, sign, side):
        if side:
            act(copy(n, i, 2))
        if sign is not None and sign <= 0:

            @pl.when(z < Z - 1)
            def _():
                act(copy(n, i, 0))

        if sign is not None and sign >= 0:

            @pl.when(z > 0)
            def _():
                act(copy(n, i, 1))

        act(copy(n, i, 3))

    def begin(act):
        for n in parts[::-1]:
            onward(act, n, me, 0, True)

    def lines(zz, sign, act, arrive):
        for n in parts:
            for yy in (y, 1 - y) if side_first[n] else (y,):
                i = index(zz, yy, c)
                if arrive is not None:
                    arrive(copy(n, i, 3))
                onward(act, n, i, sign, not side_first[n])

    def sides(zz, act, arrive, first):
        for n in parts:
            if side_first[n] == first:
                i = index(zz, 1 - y, c)
                if arrive is not None:
                    arrive(copy(n, i, 3))
                onward(act, n, i, 0 if first else None, False)

    def start(copied):
        copied.start()

    def arrived(copied):
        copied.wait_recv()

    def sent(copied):
        copied.wait_send()

    def slab(zz, sign):
        for n in parts:
            for yy in (y, 1 - y):
                arrived(copy(n, index(zz, yy, 1 - c), 3))
        if on_slab is not None:
            on_slab(zz)

    begin(start)
    sides(z, start, arrived, True)
    for stage in range(Z):
        if stage + 1 < Z:
            along(stage + 1, lambda zz, sign: lines(zz, sign, start, arrived))
        along(stage, lambda zz, sign: sides(zz, start, arrived, False))
        along(stage, slab)

    begin(sent)
    sides(z, sent, None, True)
    for stage in range(Z):
        if stage + 1 < Z:
            along(stage + 1, lambda zz, sign: lines(zz, sign, sent, None))
        along(stage, lambda zz, sign: sides(zz, sent, None, False))


def pairs(slabs):
    upper = [(i, j) for i in range(slabs) for j in range(i, slabs)]
    return upper + [(i, None) for i in range(slabs)]


def reduce_kernel(
    a_ref, d_ref, t_ref, j_ref, m_ref,
    a_buf, d_buf, total, mine, theirs, out_buf, core_buf, pair_buf, in_buf, all_buf,
    a_sem, d_sem, d_send, d_recv, x_send, x_recv, c_send, c_recv, r_send, r_recv, p_send, p_recv, m_send, m_recv,
):
    me, feat = lax.axis_index("tok"), lax.axis_index("feat")
    count = Z * Y * CORES
    group = Y * CORES

    load_a = pltpu.make_async_copy(a_ref, a_buf, a_sem)
    load_d = pltpu.make_async_copy(d_ref, d_buf.at[me], d_sem)
    load_d.start()
    load_a.start()

    barrier = pltpu.get_barrier_semaphore()
    for step in range(1, count):
        pl.semaphore_signal(
            barrier, inc=1, device_id={"tok": lax.rem(me + step, count)}, device_id_type=MESH
        )
    pl.semaphore_signal(barrier, inc=1, device_id={"feat": 1 - feat}, device_id_type=MESH)
    pl.semaphore_wait(barrier, count)
    load_d.wait()

    def swap(slab):
        return pltpu.make_async_remote_copy(
            src_ref=mine.at[slab],
            dst_ref=theirs.at[slab],
            send_sem=x_send.at[slab],
            recv_sem=x_recv.at[slab],
            device_id={"feat": 1 - feat},
            device_id_type=MESH,
        )

    def project(slab):
        total[...] = jnp.zeros_like(total)

        def part(k, carry):
            columns = pl.ds(pl.multiple_of(k * DEPTH, DEPTH), DEPTH)
            weights = d_buf[pl.ds(slab * group, group), :, columns].reshape(BLOCK, DEPTH)
            total[...] += lax.dot_general(
                a_buf[:, columns], weights, (((1,), (1,)), ((), ())), preferred_element_type=jnp.float32
            )
            return carry

        lax.fori_loop(0, a_buf.shape[1] // DEPTH, part, 0)
        mine[slab] = total[...].astype(jnp.bfloat16)
        swap(slab).start()

    load_a.wait()
    eighth = d_buf.shape[2] // 8
    views = [
        lambda i, low=low, size=size: d_buf.at[i, :, pl.ds(low * eighth, size * eighth)]
        for low, size in ((0, 3), (3, 4), (7, 1))
    ]
    spread(views, (False, False, True), d_send, d_recv, project)
    for slab in range(Z):
        swap(slab).wait()
        j_ref[slab] = (mine[slab].astype(jnp.float32) + theirs[slab].astype(jnp.float32)).astype(
            jnp.bfloat16
        )

    blocks = pairs(Z)
    half = len(blocks) // 2
    rows, chips = BLOCK // count, Z * Y
    for owner in range(2):

        @pl.when(feat == owner)
        def _():
            for n, (i, j) in enumerate(blocks[owner * half : (owner + 1) * half]):
                product = lax.dot_general(
                    t_ref[...] if j is None else j_ref[i],
                    j_ref[i if j is None else j],
                    (((0,), (0,)), ((), ())),
                    preferred_element_type=jnp.float32,
                )
                out_buf[:, :, n] = product.astype(jnp.bfloat16).reshape(CORES, chips, rows, BLOCK)

    chip, core = me // CORES, me % CORES
    between = pltpu.make_async_remote_copy(
        src_ref=out_buf.at[1 - core],
        dst_ref=core_buf,
        send_sem=c_send,
        recv_sem=c_recv,
        device_id={"tok": chip * CORES + 1 - core},
        device_id_type=MESH,
    )
    between.start()
    between.wait()
    for i in range(chips):
        pair_buf[i] = (out_buf[core, i].astype(jnp.float32) + core_buf[i].astype(jnp.float32)).astype(
            jnp.bfloat16
        )

    def part(step, slot, sem):
        other = lax.rem(chip + step, chips)
        return pltpu.make_async_remote_copy(
            src_ref=pair_buf.at[other],
            dst_ref=in_buf.at[slot],
            send_sem=r_send.at[step],
            recv_sem=r_recv.at[sem],
            device_id={"tok": other * CORES + core},
            device_id_type=MESH,
        )

    for step in range(1, chips):
        part(step, chip, chip).start()
    in_buf[chip] = pair_buf[chip]
    for step in range(1, chips):
        other = lax.rem(chip + step, chips)
        part(step, other, other).wait_recv()
    for n in range(half):
        summed = in_buf[0, n].astype(jnp.float32)
        for i in range(1, chips):
            summed += in_buf[i, n].astype(jnp.float32)
        all_buf[me, feat * half + n] = summed.astype(jnp.bfloat16)
    own = all_buf.at[me, pl.ds(feat * half, half)]
    across = pltpu.make_async_remote_copy(
        src_ref=own, dst_ref=own, send_sem=p_send, recv_sem=p_recv,
        device_id={"feat": 1 - feat}, device_id_type=MESH,
    )
    across.start()
    across.wait()
    spread([lambda i: all_buf.at[i]], (False,), m_send, m_recv, None)
    for step in range(1, chips):
        part(step, chip, chip).wait_send()
    for i in range(count):
        place = (i % CORES) * chips + i // CORES
        m_ref[:, pl.ds(place * rows, rows), :] = all_buf[i]


def reduced(activations, down_rows, target):
    count = Z * Y * CORES
    tokens, features = activations.shape
    share = down_rows.shape[0]
    blocks = len(pairs(Z))
    half, rows, chips = blocks // 2, BLOCK // count, Z * Y
    dma = pltpu.SemaphoreType.DMA
    bf16 = jnp.bfloat16
    whole = pl.BlockSpec(memory_space=pltpu.VMEM)
    return pl.pallas_call(
        reduce_kernel,
        out_shape=(
            jax.ShapeDtypeStruct((Z, tokens, BLOCK), bf16),
            jax.ShapeDtypeStruct((blocks, BLOCK, BLOCK), bf16),
        ),
        in_specs=[pl.BlockSpec(memory_space=pl.ANY)] * 2 + [whole],
        out_specs=(whole, whole),
        scratch_shapes=[
            pltpu.VMEM((tokens, features), bf16),
            pltpu.VMEM((count, share, features), bf16),
            pltpu.VMEM((tokens, BLOCK), jnp.float32),
            pltpu.VMEM((Z, tokens, BLOCK), bf16),
            pltpu.VMEM((Z, tokens, BLOCK), bf16),
            pltpu.VMEM((CORES, chips, half, rows, BLOCK), bf16),
            pltpu.VMEM((chips, half, rows, BLOCK), bf16),
            pltpu.VMEM((chips, half, rows, BLOCK), bf16),
            pltpu.VMEM((chips, half, rows, BLOCK), bf16),
            pltpu.VMEM((count, blocks, rows, BLOCK), bf16),
            dma, dma, dma((3, 4, count)), dma((3, count)), dma((Z,)), dma((Z,)), dma, dma,
            dma((chips,)), dma((chips,)), dma, dma, dma((1, 4, count)), dma((1, count)),
        ],
        compiler_params=pltpu.CompilerParams(
            collective_id=0, has_side_effects=True, vmem_limit_bytes=56 * 2**20
        ),
        cost_estimate=pl.CostEstimate(
            flops=2 * tokens * features * share * count, bytes_accessed=2 * tokens * features, transcendentals=0
        ),
    )(activations, down_rows, target)


def dot(a, b, dims, precision=None):
    return lax.dot_general(
        a, b, (dims, ((), ())), precision=precision, preferred_element_type=jnp.float32
    )


PLAIN, ACROSS = ((1,), (0,)), ((1,), (1,))
HALF = BLOCK // 2


def added(terms):
    while len(terms) > 1:
        terms = [sum(terms[i : i + 2]) for i in range(0, len(terms), 2)]
    return terms[0]


def invert_block(columns, row):
    columns = list(columns)
    for q in range(0, len(columns), 2):
        a, b = columns[q], columns[q + 1]
        a00, a10, a01, a11 = a[q : q + 1], a[q + 1 : q + 2], b[q : q + 1], b[q + 1 : q + 2]
        over = 1.0 / (a00 * a11 - a01 * a10)
        i00, i01, i10, i11 = a11 * over, -a01 * over, -a10 * over, a00 * over
        for k, column in enumerate(columns):
            if k == q:
                f0, f1, rest = i00, i10, 0.0
            elif k == q + 1:
                f0, f1, rest = i01, i11, 0.0
            else:
                x0, x1 = column[q : q + 1], column[q + 1 : q + 2]
                f0, f1, rest = i00 * x0 + i01 * x1, i10 * x0 + i11 * x1, column
            rest = rest - (a * f0 + b * f1)
            columns[k] = jnp.where(row == q, f0, jnp.where(row == q + 1, f1, rest))
    return columns


def invert(work, scaled, count):
    height = 8
    shape = (height, HALF)
    lane = lax.broadcasted_iota(jnp.int32, shape, 1)
    row = lax.broadcasted_iota(jnp.int32, shape, 0)
    square = (HALF, HALF)
    diagonal = lax.broadcasted_iota(jnp.int32, square, 0) == lax.broadcasted_iota(jnp.int32, square, 1)
    scales, tiles = [], []
    for n in range(count):
        only = jnp.where(diagonal, work[n], 0.0)
        across = lax.rsqrt(jnp.sum(only, axis=0, keepdims=True))
        down = lax.rsqrt(jnp.sum(only, axis=1, keepdims=True))
        scales.append((across, down))
        unit = work[n] * across * down
        tiles.append([unit[i : i + height] for i in range(0, HALF, height)])
    for at in range(HALF // height):
        base = at * height
        panel, done = (lane >= base) & (lane < base + height), lane < base + height
        for n in range(count):
            old = tiles[n]
            columns = {
                i: [jnp.broadcast_to(old[i][:, base + q : base + q + 1], shape) for q in range(height)]
                for i in range(at, len(old))
            }
            block = invert_block(columns[at], row)
            top = jnp.where(lane == base + row, 1.0, jnp.where(panel, 0.0, old[at]))
            left = added([block[q] * top[q : q + 1] for q in range(height)])
            work[n, pl.ds(base, height), :] = jnp.where(done, top, 0.0)
            scaled[n, pl.ds(base, height), :] = jnp.where(done, left, 0.0)
            tiles[n] = [
                jnp.where(panel, 0.0, old[i])
                - added([columns[i][q] * left[q : q + 1] for q in range(height)])
                if i > at
                else old[i]
                for i in range(len(old))
            ]
    for n in range(count):
        across, down = scales[n]
        work[n] = dot(work[n], scaled[n], ((0,), (0,)), precise) * across * down


def iterate_kernel(
    m_ref, p_ref, j_ref, t_ref, answer_ref, residual_ref,
    normal, back, direction, lift, pushed, answer, gram, systems, work, scaled, inverse, upper,
):
    feat = lax.axis_index("feat")
    blocks = pairs(Z)
    for n, (i, j) in enumerate(blocks):
        rows = slice(i * BLOCK, (i + 1) * BLOCK)
        if j is None:
            back[:, rows] = m_ref[n].astype(jnp.float32)
            continue
        columns = slice(j * BLOCK, (j + 1) * BLOCK)
        normal[rows, columns] = m_ref[n]
        if i != j:
            normal[columns, rows] = m_ref[n].T

    def gradient():
        descent = dot(back[...].astype(jnp.bfloat16), p_ref[...], PLAIN)
        return descent, dot(descent, descent, ACROSS, precise)

    def factor(count):
        def step(block, carry):
            for n in range(count):

                @pl.when(block == 0)
                def _():
                    work[n] = systems[n, :HALF, :HALF]

                @pl.when(block == 1)
                def _():
                    upper[n] = dot(inverse[0, n], systems[n, :HALF, HALF:], PLAIN, precise)
                    work[n] = systems[n, HALF:, HALF:] - dot(
                        systems[n, HALF:, :HALF], upper[n], PLAIN, precise
                    )

            invert(work, scaled, count)
            for n in range(count):
                inverse[block, n] = work[n]
            return carry

        lax.fori_loop(0, 2, step, 0)

    def solve(n, right):
        begun = dot(inverse[0, n], right[:HALF], PLAIN, precise)
        rest = right[HALF:] - dot(systems[n, HALF:, :HALF], begun, PLAIN, precise)
        lower = dot(inverse[1, n], rest, PLAIN, precise)
        return jnp.concatenate([begun - dot(upper[n], lower, PLAIN, precise), lower], axis=0)

    descent, first = gradient()
    direction[...] = descent
    gram[...] = first
    answer[...] = jnp.zeros_like(answer)

    for index in range(ITERS):
        last = index + 1 == ITERS
        lift[...] = dot(direction[...].astype(jnp.bfloat16), p_ref[...], ACROSS)
        rounded = lift[...].astype(jnp.bfloat16)
        pushed[...] = dot(rounded, normal[...], PLAIN)
        systems[0] = dot(rounded.astype(jnp.float32), pushed[...], ACROSS, precise)
        systems[1] = gram[...]
        factor(1 if last else 2)
        step_size = solve(0, gram[...]).T
        answer[...] += dot(step_size, lift[...], PLAIN, precise)
        if not last:
            back[...] -= dot(step_size, pushed[...], PLAIN, precise)
            descent, following = gradient()
            mixing = solve(1, following).T
            direction[...] = descent + dot(mixing, direction[...], PLAIN, precise)
            gram[...] = following

    fitted = jnp.zeros(residual_ref.shape, jnp.float32)
    for i in range(Z):
        fitted += dot(j_ref[i], answer[:, i * BLOCK : (i + 1) * BLOCK].astype(jnp.bfloat16), ACROSS)
    residual_ref[...] = t_ref[...].astype(jnp.float32) - fitted
    share = answer_ref.shape[0]
    answer_ref[...] = answer[:, pl.ds(pl.multiple_of(feat * share, share), share)].T


def on_block(activations, down_proj, precond, target):
    joined, sums = reduced(activations, down_proj.T, target)
    rank, wanted = precond.shape[0], target.shape[1]
    f32 = jnp.float32
    whole = pl.BlockSpec(memory_space=pltpu.VMEM)
    wide, square, small = (wanted, rank), (wanted, wanted), (2, HALF, HALF)
    return pl.pallas_call(
        iterate_kernel,
        out_shape=(
            jax.ShapeDtypeStruct((rank // lax.axis_size("feat"), wanted), f32),
            jax.ShapeDtypeStruct(target.shape, f32),
        ),
        in_specs=[whole] * 4,
        out_specs=(whole, whole),
        scratch_shapes=[
            pltpu.VMEM((rank, rank), jnp.bfloat16),
            pltpu.VMEM(wide, f32),
            pltpu.VMEM(wide, f32),
            pltpu.VMEM(wide, f32),
            pltpu.VMEM(wide, f32),
            pltpu.VMEM(wide, f32),
            pltpu.VMEM(square, f32),
            pltpu.VMEM((2,) + square, f32),
            pltpu.VMEM(small, f32),
            pltpu.VMEM(small, f32),
            pltpu.VMEM((2,) + small, f32),
            pltpu.VMEM(small, f32),
        ],
        compiler_params=pltpu.CompilerParams(vmem_limit_bytes=48 * 2**20),
    )(sums, precond, joined, target)


def solve_gram(matrix, right):
    lower = jnp.linalg.cholesky(matrix)
    middle = lax.linalg.triangular_solve(lower, right, left_side=True, lower=True)
    return lax.linalg.triangular_solve(lower, middle, left_side=True, lower=True, transpose_a=True)


def on_device(activations, down_proj, precond, target):
    feat_count = lax.axis_size("feat")
    feat_index = lax.axis_index("feat")
    share_rows = precond.shape[0] // feat_count
    partial_map = jnp.dot(
        activations,
        lax.all_gather(down_proj, "tok", axis=1, tiled=True),
        preferred_element_type=jnp.float32,
    )
    joined_share = lax.psum_scatter(partial_map, "feat", scatter_dimension=1, tiled=True).astype(
        jnp.bfloat16
    )
    row_block = lax.dynamic_slice_in_dim(precond, feat_index * share_rows, share_rows, 0)
    col_block = lax.dynamic_slice_in_dim(precond, feat_index * share_rows, share_rows, 1)

    def gradient(current):
        partial_back = lax.dot_general(
            joined_share,
            current.astype(jnp.bfloat16),
            (((0,), (0,)), ((), ())),
            preferred_element_type=jnp.float32,
        )
        summed = lax.psum(partial_back, "tok")
        gathered = lax.all_gather(summed.astype(jnp.bfloat16), "feat", axis=0, tiled=True)
        descent = lax.dot_general(
            col_block, gathered, (((0,), (0,)), ((), ())), preferred_element_type=jnp.float32
        )
        gram_matrix = lax.psum(jnp.dot(descent.T, descent, precision=precise), "feat")
        return (descent, gram_matrix)

    residual = target.astype(jnp.float32)
    descent, gram_now = gradient(residual)
    direction = descent
    solution = jnp.zeros((share_rows, target.shape[1]), jnp.float32)
    for iteration in range(ITERS):
        rounded_dir = lax.all_gather(direction.astype(jnp.bfloat16), "feat", axis=0, tiled=True)
        lift_rows = jnp.dot(row_block, rounded_dir, preferred_element_type=jnp.float32)
        partial_image = jnp.dot(
            joined_share, lift_rows.astype(jnp.bfloat16), preferred_element_type=jnp.float32
        )
        image_now = lax.psum(partial_image, "feat")
        curvature = lax.psum(jnp.dot(image_now.T, image_now, precision=precise), "tok")
        step_size = solve_gram(curvature, gram_now)
        solution = solution + jnp.dot(lift_rows, step_size, precision=precise)
        residual = residual - jnp.dot(image_now, step_size, precision=precise)
        if iteration + 1 < ITERS:
            descent, gram_next = gradient(residual)
            mixing = solve_gram(gram_now, gram_next)
            direction = descent + jnp.dot(direction, mixing, precision=precise)
            gram_now = gram_next
    return (solution, residual)


def solution(mesh):
    small = mesh.shape["tok"] == Z * Y * CORES and mesh.shape["feat"] == 2
    placed = (P("tok", "feat"), P("feat", "tok"), P(), P("tok", None))
    return jax.shard_map(
        on_block if small else on_device,
        mesh=mesh,
        in_specs=placed,
        out_specs=(P("feat", None), P("tok", None)),
        check_vma=False,
    )
```

```python
import functools

import jax
import jax.numpy as jnp
from jax import lax
from jax.experimental import pallas as pl
from jax.experimental.pallas import tpu as pltpu
from jax.sharding import PartitionSpec as P

ITERS = 2
Z, Y, CORES = 4, 2, 2
BLOCK = 256
DEPTH = 1024
MESH = pl.DeviceIdType.MESH
precise = lax.Precision.HIGHEST


def spread(views, side_first, send, recv, on_slab):
    me = lax.axis_index("tok")
    z, y, c = me // (Y * CORES), (me // CORES) % Y, me % CORES
    parts = range(len(views))

    def index(zz, yy, cc):
        return (zz * Y + yy) * CORES + cc

    targets = (me + Y * CORES, me - Y * CORES, index(z, 1 - y, c), index(z, y, 1 - c))

    def copy(n, i, way):
        return pltpu.make_async_remote_copy(
            src_ref=views[n](i),
            dst_ref=views[n](i),
            send_sem=send.at[n, way, i],
            recv_sem=recv.at[n, i],
            device_id={"tok": targets[way]},
            device_id_type=MESH,
        )

    def along(distance, visit):
        for sign in (1, -1) if distance else (0,):
            zz = z + sign * distance

            @pl.when((zz >= 0) & (zz < Z))
            def _():
                visit(zz, sign)

    def onward(act, n, i, sign, side):
        if side:
            act(copy(n, i, 2))
        if sign is not None and sign <= 0:

            @pl.when(z < Z - 1)
            def _():
                act(copy(n, i, 0))

        if sign is not None and sign >= 0:

            @pl.when(z > 0)
            def _():
                act(copy(n, i, 1))

        act(copy(n, i, 3))

    def begin(act):
        for n in parts[::-1]:
            onward(act, n, me, 0, True)

    def lines(zz, sign, act, arrive):
        for n in parts:
            for yy in (y, 1 - y) if side_first[n] else (y,):
                i = index(zz, yy, c)
                if arrive is not None:
                    arrive(copy(n, i, 3))
                onward(act, n, i, sign, not side_first[n])

    def sides(zz, act, arrive, first):
        for n in parts:
            if side_first[n] == first:
                i = index(zz, 1 - y, c)
                if arrive is not None:
                    arrive(copy(n, i, 3))
                onward(act, n, i, 0 if first else None, False)

    def start(copied):
        copied.start()

    def arrived(copied):
        copied.wait_recv()

    def sent(copied):
        copied.wait_send()

    def slab(zz, sign):
        for n in parts:
            for yy in (y, 1 - y):
                arrived(copy(n, index(zz, yy, 1 - c), 3))
        if on_slab is not None:
            on_slab(zz)

    begin(start)
    sides(z, start, arrived, True)
    for stage in range(Z):
        if stage + 1 < Z:
            along(stage + 1, lambda zz, sign: lines(zz, sign, start, arrived))
        along(stage, lambda zz, sign: sides(zz, start, arrived, False))
        along(stage, slab)

    begin(sent)
    sides(z, sent, None, True)
    for stage in range(Z):
        if stage + 1 < Z:
            along(stage + 1, lambda zz, sign: lines(zz, sign, sent, None))
        along(stage, lambda zz, sign: sides(zz, sent, None, False))


def pairs(slabs):
    upper = [(i, j) for i in range(slabs) for j in range(i, slabs)]
    return upper + [(i, None) for i in range(slabs)]


def reduce_kernel(
    a_ref, d_ref, t_ref, j_ref, m_ref,
    a_buf, d_buf, total, mine, theirs, out_buf, core_buf, pair_buf, in_buf, all_buf,
    a_sem, d_sem, d_send, d_recv, x_send, x_recv, c_send, c_recv, r_send, r_recv, p_send, p_recv, m_send, m_recv,
):
    me, feat = lax.axis_index("tok"), lax.axis_index("feat")
    count = Z * Y * CORES
    group = Y * CORES

    load_a = pltpu.make_async_copy(a_ref, a_buf, a_sem)
    load_d = pltpu.make_async_copy(d_ref, d_buf.at[me], d_sem)
    load_d.start()
    load_a.start()

    barrier = pltpu.get_barrier_semaphore()
    for step in range(1, count):
        pl.semaphore_signal(
            barrier, inc=1, device_id={"tok": lax.rem(me + step, count)}, device_id_type=MESH
        )
    pl.semaphore_signal(barrier, inc=1, device_id={"feat": 1 - feat}, device_id_type=MESH)
    pl.semaphore_wait(barrier, count)
    load_d.wait()

    def swap(slab):
        return pltpu.make_async_remote_copy(
            src_ref=mine.at[slab],
            dst_ref=theirs.at[slab],
            send_sem=x_send.at[slab],
            recv_sem=x_recv.at[slab],
            device_id={"feat": 1 - feat},
            device_id_type=MESH,
        )

    def project(slab):
        total[...] = jnp.zeros_like(total)

        def part(k, carry):
            columns = pl.ds(pl.multiple_of(k * DEPTH, DEPTH), DEPTH)
            weights = d_buf[pl.ds(slab * group, group), :, columns].reshape(BLOCK, DEPTH)
            total[...] += lax.dot_general(
                a_buf[:, columns], weights, (((1,), (1,)), ((), ())), preferred_element_type=jnp.float32
            )
            return carry

        lax.fori_loop(0, a_buf.shape[1] // DEPTH, part, 0)
        mine[slab] = total[...].astype(jnp.bfloat16)
        swap(slab).start()

    load_a.wait()
    eighth = d_buf.shape[2] // 8
    views = [
        lambda i, low=low, size=size: d_buf.at[i, :, pl.ds(low * eighth, size * eighth)]
        for low, size in ((0, 3), (3, 2), (5, 2), (7, 1))
    ]
    spread(views, (False, False, False, True), d_send, d_recv, project)
    for slab in range(Z):
        swap(slab).wait()
        j_ref[slab] = (mine[slab].astype(jnp.float32) + theirs[slab].astype(jnp.float32)).astype(
            jnp.bfloat16
        )

    blocks = pairs(Z)
    half = len(blocks) // 2
    rows, chips = BLOCK // count, Z * Y
    for owner in range(2):

        @pl.when(feat == owner)
        def _():
            for n, (i, j) in enumerate(blocks[owner * half : (owner + 1) * half]):
                product = lax.dot_general(
                    t_ref[...] if j is None else j_ref[i],
                    j_ref[i if j is None else j],
                    (((0,), (0,)), ((), ())),
                    preferred_element_type=jnp.float32,
                )
                out_buf[:, :, n] = product.astype(jnp.bfloat16).reshape(CORES, chips, rows, BLOCK)

    chip, core = me // CORES, me % CORES
    between = pltpu.make_async_remote_copy(
        src_ref=out_buf.at[1 - core],
        dst_ref=core_buf,
        send_sem=c_send,
        recv_sem=c_recv,
        device_id={"tok": chip * CORES + 1 - core},
        device_id_type=MESH,
    )
    between.start()
    between.wait()
    for i in range(chips):
        pair_buf[i] = (out_buf[core, i].astype(jnp.float32) + core_buf[i].astype(jnp.float32)).astype(
            jnp.bfloat16
        )

    def part(step, slot, sem):
        other = lax.rem(chip + step, chips)
        return pltpu.make_async_remote_copy(
            src_ref=pair_buf.at[other],
            dst_ref=in_buf.at[slot],
            send_sem=r_send.at[step],
            recv_sem=r_recv.at[sem],
            device_id={"tok": other * CORES + core},
            device_id_type=MESH,
        )

    for step in range(1, chips):
        part(step, chip, chip).start()
    in_buf[chip] = pair_buf[chip]
    for step in range(1, chips):
        other = lax.rem(chip + step, chips)
        part(step, other, other).wait_recv()
    for n in range(half):
        summed = in_buf[0, n].astype(jnp.float32)
        for i in range(1, chips):
            summed += in_buf[i, n].astype(jnp.float32)
        all_buf[me, feat * half + n] = summed.astype(jnp.bfloat16)
    own = all_buf.at[me, pl.ds(feat * half, half)]
    across = pltpu.make_async_remote_copy(
        src_ref=own, dst_ref=own, send_sem=p_send, recv_sem=p_recv,
        device_id={"feat": 1 - feat}, device_id_type=MESH,
    )
    across.start()
    across.wait()
    spread([lambda i: all_buf.at[i]], (False,), m_send, m_recv, None)
    for step in range(1, chips):
        part(step, chip, chip).wait_send()
    for i in range(count):
        place = (i % CORES) * chips + i // CORES
        m_ref[:, pl.ds(place * rows, rows), :] = all_buf[i]


def reduced(activations, down_rows, target):
    count = Z * Y * CORES
    tokens, features = activations.shape
    share = down_rows.shape[0]
    blocks = len(pairs(Z))
    half, rows, chips = blocks // 2, BLOCK // count, Z * Y
    dma = pltpu.SemaphoreType.DMA
    bf16 = jnp.bfloat16
    whole = pl.BlockSpec(memory_space=pltpu.VMEM)
    return pl.pallas_call(
        reduce_kernel,
        out_shape=(
            jax.ShapeDtypeStruct((Z, tokens, BLOCK), bf16),
            jax.ShapeDtypeStruct((blocks, BLOCK, BLOCK), bf16),
        ),
        in_specs=[pl.BlockSpec(memory_space=pl.ANY)] * 2 + [whole],
        out_specs=(whole, whole),
        scratch_shapes=[
            pltpu.VMEM((tokens, features), bf16),
            pltpu.VMEM((count, share, features), bf16),
            pltpu.VMEM((tokens, BLOCK), jnp.float32),
            pltpu.VMEM((Z, tokens, BLOCK), bf16),
            pltpu.VMEM((Z, tokens, BLOCK), bf16),
            pltpu.VMEM((CORES, chips, half, rows, BLOCK), bf16),
            pltpu.VMEM((chips, half, rows, BLOCK), bf16),
            pltpu.VMEM((chips, half, rows, BLOCK), bf16),
            pltpu.VMEM((chips, half, rows, BLOCK), bf16),
            pltpu.VMEM((count, blocks, rows, BLOCK), bf16),
            dma, dma, dma((4, 4, count)), dma((4, count)), dma((Z,)), dma((Z,)), dma, dma,
            dma((chips,)), dma((chips,)), dma, dma, dma((1, 4, count)), dma((1, count)),
        ],
        compiler_params=pltpu.CompilerParams(
            collective_id=0, has_side_effects=True, vmem_limit_bytes=56 * 2**20
        ),
        cost_estimate=pl.CostEstimate(
            flops=2 * tokens * features * share * count, bytes_accessed=2 * tokens * features, transcendentals=0
        ),
    )(activations, down_rows, target)


def dot(a, b, dims, precision=None):
    return lax.dot_general(
        a, b, (dims, ((), ())), precision=precision, preferred_element_type=jnp.float32
    )


PLAIN, ACROSS = ((1,), (0,)), ((1,), (1,))
HALF = BLOCK // 2


def added(terms):
    while len(terms) > 1:
        terms = [sum(terms[i : i + 2]) for i in range(0, len(terms), 2)]
    return terms[0]


def invert_block(columns, row):
    columns = list(columns)
    for q in range(0, len(columns), 2):
        a, b = columns[q], columns[q + 1]
        a00, a10, a01, a11 = a[q : q + 1], a[q + 1 : q + 2], b[q : q + 1], b[q + 1 : q + 2]
        over = 1.0 / (a00 * a11 - a01 * a10)
        i00, i01, i10, i11 = a11 * over, -a01 * over, -a10 * over, a00 * over
        for k, column in enumerate(columns):
            if k == q:
                f0, f1, rest = i00, i10, 0.0
            elif k == q + 1:
                f0, f1, rest = i01, i11, 0.0
            else:
                x0, x1 = column[q : q + 1], column[q + 1 : q + 2]
                f0, f1, rest = i00 * x0 + i01 * x1, i10 * x0 + i11 * x1, column
            rest = rest - (a * f0 + b * f1)
            columns[k] = jnp.where(row == q, f0, jnp.where(row == q + 1, f1, rest))
    return columns


def invert(work, scaled, count):
    height = 8
    shape = (height, HALF)
    lane = lax.broadcasted_iota(jnp.int32, shape, 1)
    row = lax.broadcasted_iota(jnp.int32, shape, 0)
    square = (HALF, HALF)
    diagonal = lax.broadcasted_iota(jnp.int32, square, 0) == lax.broadcasted_iota(jnp.int32, square, 1)
    scales, tiles = [], []
    for n in range(count):
        only = jnp.where(diagonal, work[n], 0.0)
        across = lax.rsqrt(jnp.sum(only, axis=0, keepdims=True))
        down = lax.rsqrt(jnp.sum(only, axis=1, keepdims=True))
        scales.append((across, down))
        unit = work[n] * across * down
        tiles.append([unit[i : i + height] for i in range(0, HALF, height)])
    for at in range(HALF // height):
        base = at * height
        panel, done = (lane >= base) & (lane < base + height), lane < base + height
        for n in range(count):
            old = tiles[n]
            columns = {
                i: [jnp.broadcast_to(old[i][:, base + q : base + q + 1], shape) for q in range(height)]
                for i in range(at, len(old))
            }
            block = invert_block(columns[at], row)
            top = jnp.where(lane == base + row, 1.0, jnp.where(panel, 0.0, old[at]))
            left = added([block[q] * top[q : q + 1] for q in range(height)])
            work[n, pl.ds(base, height), :] = jnp.where(done, top, 0.0)
            scaled[n, pl.ds(base, height), :] = jnp.where(done, left, 0.0)
            tiles[n] = [
                jnp.where(panel, 0.0, old[i])
                - added([columns[i][q] * left[q : q + 1] for q in range(height)])
                if i > at
                else old[i]
                for i in range(len(old))
            ]
    for n in range(count):
        across, down = scales[n]
        work[n] = dot(work[n], scaled[n], ((0,), (0,)), precise) * across * down


def iterate_kernel(
    m_ref, p_ref, j_ref, t_ref, answer_ref, residual_ref,
    normal, back, direction, lift, pushed, answer, gram, systems, work, scaled, inverse, upper, j_buf, j_sem,
):
    feat = lax.axis_index("feat")
    load_j = pltpu.make_async_copy(j_ref, j_buf, j_sem)
    load_j.start()
    blocks = pairs(Z)
    for n, (i, j) in enumerate(blocks):
        rows = slice(i * BLOCK, (i + 1) * BLOCK)
        if j is None:
            back[:, rows] = m_ref[n].astype(jnp.float32)
            continue
        columns = slice(j * BLOCK, (j + 1) * BLOCK)
        normal[rows, columns] = m_ref[n]
        if i != j:
            normal[columns, rows] = m_ref[n].T

    def gradient():
        descent = dot(back[...].astype(jnp.bfloat16), p_ref[...], PLAIN)
        return descent, dot(descent, descent, ACROSS, precise)

    def factor(count):
        def step(block, carry):
            for n in range(count):

                @pl.when(block == 0)
                def _():
                    work[n] = systems[n, :HALF, :HALF]

                @pl.when(block == 1)
                def _():
                    upper[n] = dot(inverse[0, n], systems[n, :HALF, HALF:], PLAIN, precise)
                    work[n] = systems[n, HALF:, HALF:] - dot(
                        systems[n, HALF:, :HALF], upper[n], PLAIN, precise
                    )

            invert(work, scaled, count)
            for n in range(count):
                inverse[block, n] = work[n]
            return carry

        lax.fori_loop(0, 2, step, 0)

    def solve(n, right):
        begun = dot(inverse[0, n], right[:HALF], PLAIN, precise)
        rest = right[HALF:] - dot(systems[n, HALF:, :HALF], begun, PLAIN, precise)
        lower = dot(inverse[1, n], rest, PLAIN, precise)
        return jnp.concatenate([begun - dot(upper[n], lower, PLAIN, precise), lower], axis=0)

    descent, first = gradient()
    direction[...] = descent
    gram[...] = first
    answer[...] = jnp.zeros_like(answer)

    for index in range(ITERS):
        last = index + 1 == ITERS
        lift[...] = dot(direction[...].astype(jnp.bfloat16), p_ref[...], ACROSS)
        rounded = lift[...].astype(jnp.bfloat16)
        pushed[...] = dot(rounded, normal[...], PLAIN)
        systems[0] = dot(rounded.astype(jnp.float32), pushed[...], ACROSS, precise)
        systems[1] = gram[...]
        factor(1 if last else 2)
        step_size = solve(0, gram[...]).T
        answer[...] += dot(step_size, lift[...], PLAIN, precise)
        if not last:
            back[...] -= dot(step_size, pushed[...], PLAIN, precise)
            descent, following = gradient()
            mixing = solve(1, following).T
            direction[...] = descent + dot(mixing, direction[...], PLAIN, precise)
            gram[...] = following

    load_j.wait()
    fitted = jnp.zeros(residual_ref.shape, jnp.float32)
    for i in range(Z):
        fitted += dot(j_buf[i], answer[:, i * BLOCK : (i + 1) * BLOCK].astype(jnp.bfloat16), ACROSS)
    residual_ref[...] = t_ref[...].astype(jnp.float32) - fitted
    share = answer_ref.shape[0]
    answer_ref[...] = answer[:, pl.ds(pl.multiple_of(feat * share, share), share)].T


def on_block(activations, down_proj, precond, target):
    joined, sums = reduced(activations, down_proj.T, target)
    rank, wanted = precond.shape[0], target.shape[1]
    f32 = jnp.float32
    whole = pl.BlockSpec(memory_space=pltpu.VMEM)
    wide, square, small = (wanted, rank), (wanted, wanted), (2, HALF, HALF)
    return pl.pallas_call(
        iterate_kernel,
        out_shape=(
            jax.ShapeDtypeStruct((rank // lax.axis_size("feat"), wanted), f32),
            jax.ShapeDtypeStruct(target.shape, f32),
        ),
        in_specs=[whole, whole, pl.BlockSpec(memory_space=pl.ANY), whole],
        out_specs=(whole, whole),
        scratch_shapes=[
            pltpu.VMEM((rank, rank), jnp.bfloat16),
            pltpu.VMEM(wide, f32),
            pltpu.VMEM(wide, f32),
            pltpu.VMEM(wide, f32),
            pltpu.VMEM(wide, f32),
            pltpu.VMEM(wide, f32),
            pltpu.VMEM(square, f32),
            pltpu.VMEM((2,) + square, f32),
            pltpu.VMEM(small, f32),
            pltpu.VMEM(small, f32),
            pltpu.VMEM((2,) + small, f32),
            pltpu.VMEM(small, f32),
            pltpu.VMEM(joined.shape, joined.dtype),
            pltpu.SemaphoreType.DMA,
        ],
        compiler_params=pltpu.CompilerParams(vmem_limit_bytes=48 * 2**20),
    )(sums, precond, joined, target)


def solve_gram(matrix, right):
    lower = jnp.linalg.cholesky(matrix)
    middle = lax.linalg.triangular_solve(lower, right, left_side=True, lower=True)
    return lax.linalg.triangular_solve(lower, middle, left_side=True, lower=True, transpose_a=True)


def on_device(activations, down_proj, precond, target):
    feat_count = lax.axis_size("feat")
    feat_index = lax.axis_index("feat")
    share_rows = precond.shape[0] // feat_count
    partial_map = jnp.dot(
        activations,
        lax.all_gather(down_proj, "tok", axis=1, tiled=True),
        preferred_element_type=jnp.float32,
    )
    joined_share = lax.psum_scatter(partial_map, "feat", scatter_dimension=1, tiled=True).astype(
        jnp.bfloat16
    )
    row_block = lax.dynamic_slice_in_dim(precond, feat_index * share_rows, share_rows, 0)
    col_block = lax.dynamic_slice_in_dim(precond, feat_index * share_rows, share_rows, 1)

    def gradient(current):
        partial_back = lax.dot_general(
            joined_share,
            current.astype(jnp.bfloat16),
            (((0,), (0,)), ((), ())),
            preferred_element_type=jnp.float32,
        )
        summed = lax.psum(partial_back, "tok")
        gathered = lax.all_gather(summed.astype(jnp.bfloat16), "feat", axis=0, tiled=True)
        descent = lax.dot_general(
            col_block, gathered, (((0,), (0,)), ((), ())), preferred_element_type=jnp.float32
        )
        gram_matrix = lax.psum(jnp.dot(descent.T, descent, precision=precise), "feat")
        return (descent, gram_matrix)

    residual = target.astype(jnp.float32)
    descent, gram_now = gradient(residual)
    direction = descent
    solution = jnp.zeros((share_rows, target.shape[1]), jnp.float32)
    for iteration in range(ITERS):
        rounded_dir = lax.all_gather(direction.astype(jnp.bfloat16), "feat", axis=0, tiled=True)
        lift_rows = jnp.dot(row_block, rounded_dir, preferred_element_type=jnp.float32)
        partial_image = jnp.dot(
            joined_share, lift_rows.astype(jnp.bfloat16), preferred_element_type=jnp.float32
        )
        image_now = lax.psum(partial_image, "feat")
        curvature = lax.psum(jnp.dot(image_now.T, image_now, precision=precise), "tok")
        step_size = solve_gram(curvature, gram_now)
        solution = solution + jnp.dot(lift_rows, step_size, precision=precise)
        residual = residual - jnp.dot(image_now, step_size, precision=precise)
        if iteration + 1 < ITERS:
            descent, gram_next = gradient(residual)
            mixing = solve_gram(gram_now, gram_next)
            direction = descent + jnp.dot(direction, mixing, precision=precise)
            gram_now = gram_next
    return (solution, residual)


def solution(mesh):
    small = mesh.shape["tok"] == Z * Y * CORES and mesh.shape["feat"] == 2
    placed = (P("tok", "feat"), P("feat", "tok"), P(), P("tok", None))
    return jax.shard_map(
        on_block if small else on_device,
        mesh=mesh,
        in_specs=placed,
        out_specs=(P("feat", None), P("tok", None)),
        check_vma=False,
    )
```
